128 devices in a mesh: gx: 16 (over z, y), gy: 8 (over x, core).
Axes of the slice: x: 4, y: 4, z: 4, core: 2. Of those that a mesh axis runs over, the one named last changes fastest.
Arguments:
- enthalpy: float32 [1024, 1024, 128], P('gx', 'gy'), may hold values from 0 to 2.5
- conductivity: float32 [1024, 1024, 128], P('gx', 'gy'), may hold values from 0.5 to 1.5
- bead_enthalpy: float32 [1024, 1024, 128], P('gx', 'gy'), may hold values from 2 to 3
- birth_time: int32 [1024, 1024, 128], P('gx', 'gy'), may hold values from -2000 to 7999
- send_rows: int32 [16, 8, 128, 32], P('gx', 'gy'), may hold values from 0 to 8191
- send_counts: int32 [16, 8, 128], P('gx', 'gy'), may hold values from 0 to 32, as said below
Outputs:
- enthalpy_end: float32 [1024, 1024, 128], P('gx', 'gy')
- owner_rows: float32 [524288, 128], P(('gx', 'gy'))
The draws below stay inside these ranges and needn't reach their ends.
Inputs may be any that keep to these rules, and one draw needn't show every extreme that they name: `send_counts`: in every draw one owner receives 32 rows from every tile.
All inputs are finite; a program needn't handle non-finite values.
Results may differ from the reference program's by a relative error of at most 0.0003.
Values sent between devices are 32-bit elements; how exact they have to be, the bound alone decides.
No kernel may reach another device: no remote copies, remote signals or barrier semaphores. Data moves between devices by JAX's collectives and lax.ppermute only.
A program may use at most 192 MiB of HBM per device.

```python
import jax
import jax.numpy as jnp

BLOCK_TRACK_N = 64
BLOCK_LATERAL_N = 128
STACK_POINTS = 128
STEPS = 3
TICKS = 2000
CAP = 32
NX = 1024
NY = 1024
OWNERS = 128
N_GX = 16
N_GY = 8


def draw_send_counts(key, part):
    first_key = jax.random.fold_in(key, 11)
    second_key = jax.random.fold_in(key, 23)
    blocks_track_count = NX // BLOCK_TRACK_N
    blocks_lateral_count = NY // BLOCK_LATERAL_N
    counts = jax.random.randint(first_key, (blocks_track_count, blocks_lateral_count, OWNERS), 0, CAP + 1, dtype=jnp.int32)
    full_owner = jax.random.randint(second_key, (), 0, OWNERS, dtype=jnp.int32)
    owner_index = jnp.arange(OWNERS, dtype=jnp.int32)
    return jnp.where(owner_index[None, None, :] == full_owner, CAP, counts).astype(jnp.int32)


def with_ends(entries, stream_key, low, top_value):
    dims = entries.shape
    place = [jax.random.randint(jax.random.fold_in(stream_key, axis), (), 0, dims[axis]) for axis in range(len(dims))]
    entries = entries.at[tuple(place)].set(low)
    longest = dims.index(max(dims))
    place[longest] = (place[longest] + 1) % dims[longest]
    return entries.at[tuple(place)].set(top_value)


def block_levels(stream_key, dims, cuts, least, top_value):
    factor_of, own = 1.0, jax.random.fold_in(stream_key, 6)
    for dim, blocks in cuts:
        heights = jnp.exp(jax.random.uniform(jax.random.fold_in(own, dim), (blocks,), jnp.float32, least / len(cuts), top_value / len(cuts)))
        factor_of = factor_of * jnp.repeat(heights, dims[dim] // blocks).reshape([-1 if axis == dim else 1 for axis in range(len(dims))])
    return factor_of


def setup_inputs(seed: int = 0) -> dict:
    streams_of = jax.random.split(jax.random.key(seed), 7)
    enthalpy = jnp.clip(2.5 * jax.random.uniform(streams_of[0], (NX, NY, STACK_POINTS), jnp.float32) ** block_levels(streams_of[0], (NX, NY, STACK_POINTS), ((0, 16), (1, 8)), -0.2, 0.2), 0.0, 2.5)
    conductivity = jnp.clip(0.5 + 1.0 * jax.random.uniform(streams_of[1], (NX, NY, STACK_POINTS), jnp.float32) ** block_levels(streams_of[1], (NX, NY, STACK_POINTS), ((0, 16), (1, 8)), -0.2, 0.2), 0.5, 1.5)
    bead_enthalpy = jnp.clip(2.0 + 1.0 * jax.random.uniform(streams_of[2], (NX, NY, STACK_POINTS), jnp.float32) ** block_levels(streams_of[2], (NX, NY, STACK_POINTS), ((0, 16), (1, 8)), -0.2, 0.2), 2.0, 3.0)
    birth_time = with_ends(jax.random.randint(streams_of[3], (NX, NY, STACK_POINTS), -TICKS, (STEPS + 1) * TICKS), jax.random.fold_in(streams_of[3], 1), -TICKS, ((STEPS + 1) * TICKS) - 1).astype(jnp.int32)
    send_rows = with_ends(jax.random.randint(streams_of[4], (N_GX, N_GY, OWNERS, CAP), 0, BLOCK_TRACK_N * BLOCK_LATERAL_N), jax.random.fold_in(streams_of[4], 1), 0, (BLOCK_TRACK_N * BLOCK_LATERAL_N) - 1).astype(jnp.int32)
    send_counts = draw_send_counts(jax.random.fold_in(streams_of[6], 71), 0)
    return dict(enthalpy=enthalpy, conductivity=conductivity, bead_enthalpy=bead_enthalpy, birth_time=birth_time, send_rows=send_rows, send_counts=send_counts)


LATENT = 0.5
RATE = 0.08


def heat_content_into_kelvin(heat_content_latest):
    return jnp.minimum(heat_content_latest, 1.0) + jnp.maximum(heat_content_latest - 1.0 - LATENT, 0.0)


def face_flux(c_one, c_two, a_one, a_two, t_one, t_two):
    return 2.0 * c_one * c_two / (c_one + c_two) * (a_one * a_two) * (t_two - t_one)


def advance(enthalpy_pad, bordered_diffusivity, bead_pad, birth_pad, inside, step):
    in_grid = inside > 0.5
    born_now = in_grid & (birth_pad >= float(step * TICKS)) & (birth_pad < float((step + 1) * TICKS))
    present_heat_content = jnp.where(born_now, bead_pad, enthalpy_pad)
    standing_share = jnp.clip(float(step + 1) - birth_pad / float(TICKS), 0.0, 1.0)
    active = jnp.where(in_grid, standing_share, 0.0).astype(jnp.float32)
    kelvin_grid_values = heat_content_into_kelvin(present_heat_content)
    heat_diffusivity_grid = bordered_diffusivity * (0.5 + 0.25 * kelvin_grid_values)
    c_mid = heat_diffusivity_grid[1:-1, 1:-1]
    a_mid = active[1:-1, 1:-1]
    central_kelvin_value = kelvin_grid_values[1:-1, 1:-1]
    net_flux = jnp.zeros(c_mid.shape, jnp.float32)
    cuts = ((slice(2, None), slice(1, -1)), (slice(None, -2), slice(1, -1)),
            (slice(1, -1), slice(2, None)), (slice(1, -1), slice(None, -2)))
    for track_limit_index, lateral_limit_index in cuts:
        net_flux = net_flux + face_flux(c_mid, heat_diffusivity_grid[track_limit_index, lateral_limit_index], a_mid, active[track_limit_index, lateral_limit_index],
                                        central_kelvin_value, kelvin_grid_values[track_limit_index, lateral_limit_index])
    z_flux = face_flux(c_mid[..., :-1], c_mid[..., 1:], a_mid[..., :-1], a_mid[..., 1:],
                       central_kelvin_value[..., :-1], central_kelvin_value[..., 1:])
    z_edge = jnp.zeros(z_flux.shape[:-1] + (1,), jnp.float32)
    net_flux = net_flux + jnp.concatenate([z_flux, z_edge], -1) - jnp.concatenate([z_edge, z_flux], -1)
    return present_heat_content[1:-1, 1:-1] + RATE * net_flux


def pad_plane(array):
    return jnp.pad(array, ((1, 1), (1, 1), (0, 0)))


def reference(enthalpy, conductivity, bead_enthalpy, birth_time, send_rows, send_counts):
    inside = pad_plane(jnp.ones_like(enthalpy))
    bordered_diffusivity = jnp.where(inside > 0.5, pad_plane(conductivity), 1.0)
    bead_pad = pad_plane(bead_enthalpy)
    birth_pad = pad_plane(birth_time.astype(jnp.float32))
    present_heat_content = enthalpy
    for step in range(STEPS):
        present_heat_content = advance(pad_plane(present_heat_content), bordered_diffusivity, bead_pad, birth_pad, inside, step)
    kelvin_grid_values = heat_content_into_kelvin(present_heat_content)
    blocks_track_count = NX // BLOCK_TRACK_N
    blocks_lateral_count = NY // BLOCK_LATERAL_N
    integration_point_matrix = kelvin_grid_values.reshape(blocks_track_count, BLOCK_TRACK_N, blocks_lateral_count, BLOCK_LATERAL_N, STACK_POINTS).transpose(0, 2, 1, 3, 4)
    integration_point_matrix = integration_point_matrix.reshape(blocks_track_count, blocks_lateral_count, BLOCK_TRACK_N * BLOCK_LATERAL_N, STACK_POINTS)
    picked = jax.vmap(jax.vmap(lambda table, rows: table[rows]))(integration_point_matrix, send_rows)
    slot_index = jnp.arange(CAP, dtype=jnp.int32)
    keep_slot = slot_index[None, None, None, :] < send_counts[..., None]
    picked = jnp.where(keep_slot[..., None], picked, 0.0)
    picked = picked.reshape(OWNERS, OWNERS, CAP, STACK_POINTS).transpose(1, 0, 2, 3).reshape(OWNERS * OWNERS * CAP, STACK_POINTS)
    return present_heat_content, picked
```

```python
import functools

import jax
import jax.numpy as jnp
from jax import lax
from jax.experimental import pallas as pl
from jax.experimental.pallas import tpu as pltpu
from jax.sharding import PartitionSpec as P

STEPS = 3
TICKS = 2000
LATENT = 0.5
SHARE = 0.2
TICK_SHARE = SHARE / TICKS

HALO = 3
EDGE = 8
CHUNKS = 4


def kelvin(h):
    return jnp.minimum(h, jnp.maximum(h - LATENT, 1.0))


def face(one, two):
    t_one, c_one, p_one = one
    t_two, c_two, p_two = two
    return p_one * p_two * pl.reciprocal(c_one + c_two, approx=True) * (t_two - t_one)


def window_kernel(
    track, lateral, index_ref, h_hbm, k_hbm, bead_hbm, birth_hbm, xlo_ref, xhi_ref, ylo_ref, yhi_ref,
    clo_ref, chi_ref, out_hbm, rows_ref, hs, ks, bs, bead_v, birth_v, ring_t, ring_c, ring_p, fx_s,
    fy_s, sem_in, sem_out,
):
    planes = track + 2 * HALO
    height = lateral + 2 * EDGE
    ring = height + 2 * EDGE
    piece = track // CHUNKS

    def copies(n):
        src = pl.ds(n * piece, piece)
        dst = pl.ds(HALO + n * piece, piece)
        return [
            pltpu.make_async_copy(h_hbm.at[src], hs.at[dst, pl.ds(EDGE, lateral)], sem_in.at[0, n]),
            pltpu.make_async_copy(k_hbm.at[src], ks.at[dst, pl.ds(EDGE, lateral)], sem_in.at[1, n]),
            pltpu.make_async_copy(bead_hbm.at[src], bead_v.at[src], sem_in.at[2, n]),
            pltpu.make_async_copy(birth_hbm.at[src], birth_v.at[src], sem_in.at[3, n]),
        ]

    for n in range(CHUNKS):
        for copy in copies(n):
            copy.start()

    def place(h, k, b, x, rows):
        inside = k > 0.0
        hs[x, rows, :] = h
        ks[x, rows, :] = jnp.where(inside, k, 1.0)
        bs[x, rows, :] = jnp.where(inside, b, 1.0)

    for ref, first in ((xlo_ref, 0), (xhi_ref, HALO + track)):
        for d in range(HALO):
            place(ref[d], ref[HALO + d], ref[2 * HALO + d], first + d, pl.ds(EDGE, lateral))
    for ref, first in ((ylo_ref, EDGE - HALO), (yhi_ref, EDGE + lateral)):
        @pl.loop(0, track)
        def _(x, ref=ref, first=first):
            place(ref[x, 0:HALO], ref[x, HALO:2 * HALO], ref[x, 2 * HALO:], x + HALO, pl.ds(first, HALO))
    for ref, first in ((clo_ref, 0), (chi_ref, HALO + track)):
        for d in range(HALO):
            for side, row in ((0, EDGE - HALO), (1, EDGE + lateral)):
                at = side * 3 * HALO
                place(
                    ref[d, at:at + HALO], ref[d, at + HALO:at + 2 * HALO], ref[d, at + 2 * HALO:at + 3 * HALO],
                    first + d, pl.ds(row, HALO),
                )

    for n in range(CHUNKS):
        for copy in copies(n):
            copy.wait()

        @pl.loop(n * piece, (n + 1) * piece)
        def _(x):
            birth = birth_v[x]
            rows = pl.ds(EDGE, lateral)
            born = (birth >= 0) & (birth < STEPS * TICKS)
            hs[x + HALO, rows, :] = jnp.where(born, bead_v[x], hs[x + HALO, rows, :])
            bs[x + HALO, rows, :] = birth.astype(jnp.float32) * TICK_SHARE

    def run_step(step, xa, xb, r0, r1, size):
        def point(x, r, n):
            rows = pl.ds(r, n)
            t = kelvin(hs[x, rows, :])
            c = ks[x, rows, :] * (2.0 + t)
            a = jnp.clip(SHARE * (step + 1) - bs[x, rows, :], 0.0, SHARE)
            return t, c, c * a

        def slot(x):
            return pl.multiple_of(lax.rem(x, 2) * ring + EDGE, EDGE)

        def put(at, values):
            for ref, value in zip((ring_t, ring_c, ring_p), values):
                ref[at, :] = value

        def get(at):
            return ring_t[at, :], ring_c[at, :], ring_p[at, :]

        starts = list(range(r0, r1, size))
        ends = [r for r in (r0 - EDGE, r1) if 0 <= r < height]
        for r in starts + ends:
            n = size if r in starts else EDGE
            before = point(xa - 1, r, n)
            now = point(xa, r, n)
            put(pl.ds(slot(jnp.int32(xa)) + r, n), now)
            fx_s[pl.ds(r, n), :] = face(before, now)

        @pl.loop(xa, xb)
        def _(x):
            here, there = slot(x), slot(x + 1)
            keep = lax.broadcasted_iota(jnp.int32, (size, 128), 1) < 127
            for r in ends:
                put(pl.ds(there + r, EDGE), point(x + 1, r, EDGE))
            if r0 > 0:
                at = here + r0 - EDGE
                fy_s[pl.ds(at, EDGE), :] = face(get(pl.ds(at, EDGE)), get(pl.ds(at + 1, EDGE)))
            for r in starts:
                cur = get(pl.ds(here + r, size))
                nxt = point(x + 1, r, size)
                put(pl.ds(there + r, size), nxt)
                fx = face(cur, nxt)
                fx_old = fx_s[pl.ds(r, size), :]
                fx_s[pl.ds(r, size), :] = fx
                fy = face(cur, get(pl.ds(here + r + 1, size)))
                fy_s[pl.ds(here + r, size), :] = fy
                fy_old = fy_s[pl.ds(here + r - 1, size), :]
                up = [pltpu.roll(v, 127, 1) for v in cur]
                up[2] = jnp.where(keep, up[2], 0.0)
                fz = face(cur, up)
                flux = (fx - fx_old) + (fy - fy_old) + (fz - pltpu.roll(fz, 1, 1))
                hs[x, pl.ds(r, size), :] = hs[x, pl.ds(r, size), :] + flux

    run_step(0, 1, planes - 1, 0, height, 24)
    run_step(1, 2, planes - 2, 0, height, 24)

    def out_copy(n):
        return pltpu.make_async_copy(
            hs.at[pl.ds(HALO + n * piece, piece), pl.ds(EDGE, lateral)],
            out_hbm.at[pl.ds(n * piece, piece)],
            sem_out.at[n],
        )

    run_step(2, HALO, HALO + track, EDGE, EDGE + lateral, 32)
    for n in range(CHUNKS):
        out_copy(n).start()

    hs[0, 0:EDGE, :] = jnp.zeros((EDGE, 128), jnp.float32)
    owners, slots = index_ref.shape
    flat = hs.reshape(planes * height, 128)

    @pl.loop(0, owners)
    def _(o):
        for k in range(slots):
            rows_ref[pl.ds(o * slots + k, 1), :] = kelvin(flat[pl.ds(index_ref[o, k], 1), :])

    for n in range(CHUNKS):
        out_copy(n).wait()


def window(index, h, k, bead, birth, halos):
    track, lateral, stack = h.shape
    planes, height = track + 2 * HALO, lateral + 2 * EDGE
    ring = height + 2 * EDGE
    owners, slots = index.shape
    anyspace = pl.BlockSpec(memory_space=pl.ANY)
    vmem = pl.BlockSpec(memory_space=pltpu.VMEM)
    grid_shape = (planes, height, stack)
    return pl.pallas_call(
        functools.partial(window_kernel, track, lateral),
        out_shape=(
            jax.ShapeDtypeStruct(h.shape, jnp.float32),
            jax.ShapeDtypeStruct((owners * slots, stack), jnp.float32),
        ),
        in_specs=[pl.BlockSpec(memory_space=pltpu.SMEM)] + [anyspace] * 4 + [vmem] * 6,
        out_specs=(anyspace, vmem),
        scratch_shapes=[
            pltpu.VMEM(grid_shape, jnp.float32),
            pltpu.VMEM(grid_shape, jnp.float32),
            pltpu.VMEM(grid_shape, jnp.float32),
            pltpu.VMEM(h.shape, jnp.float32),
            pltpu.VMEM(h.shape, jnp.int32),
            pltpu.VMEM((2 * ring, stack), jnp.float32),
            pltpu.VMEM((2 * ring, stack), jnp.float32),
            pltpu.VMEM((2 * ring, stack), jnp.float32),
            pltpu.VMEM((height, stack), jnp.float32),
            pltpu.VMEM((2 * ring, stack), jnp.float32),
            pltpu.SemaphoreType.DMA((4, CHUNKS)),
            pltpu.SemaphoreType.DMA((CHUNKS,)),
        ],
        compiler_params=pltpu.CompilerParams(vmem_limit_bytes=50 * 1024 * 1024),
    )(index, h, k, bead, birth, *halos)


def shift(axis, by):
    count = lax.axis_size(axis)
    return [(i, i + by) for i in range(count) if 0 <= i + by < count]


def per_device(enthalpy, conductivity, bead_enthalpy, birth_time, send_rows, send_counts):
    track, lateral, _ = enthalpy.shape

    def fields(cut):
        birth = birth_time[cut]
        born = (birth >= 0) & (birth < STEPS * TICKS)
        return (
            jnp.where(born, bead_enthalpy[cut], enthalpy[cut]),
            conductivity[cut],
            birth.astype(jnp.float32) * TICK_SHARE,
        )

    low, high = slice(0, HALO), slice(-HALO, None)
    xlo = lax.ppermute(jnp.concatenate(fields((high,)), 0), "gx", shift("gx", 1))
    xhi = lax.ppermute(jnp.concatenate(fields((low,)), 0), "gx", shift("gx", -1))
    ylo = lax.ppermute(jnp.concatenate(fields((slice(None), high)), 1), "gy", shift("gy", 1))
    yhi = lax.ppermute(jnp.concatenate(fields((slice(None), low)), 1), "gy", shift("gy", -1))
    clo = lax.ppermute(jnp.concatenate([ylo[-HALO:], yhi[-HALO:]], 1), "gx", shift("gx", 1))
    chi = lax.ppermute(jnp.concatenate([ylo[:HALO], yhi[:HALO]], 1), "gx", shift("gx", -1))

    rows, counts = send_rows[0, 0], send_counts[0, 0]
    slot = jnp.arange(rows.shape[1], dtype=jnp.int32)
    place = (rows // lateral + HALO) * (lateral + 2 * EDGE) + rows % lateral + EDGE
    index = jnp.where(slot[None, :] < counts[:, None], place, 0)
    end, outgoing = window(
        index, enthalpy, conductivity, bead_enthalpy, birth_time, (xlo, xhi, ylo, yhi, clo, chi)
    )
    outgoing = outgoing.reshape(rows.shape + outgoing.shape[1:])
    received = lax.all_to_all(outgoing, ("gx", "gy"), split_axis=0, concat_axis=0, tiled=True)
    return end, received.reshape(-1, received.shape[-1])


def solution(mesh):
    in_specs = (
        P("gx", "gy", None),
        P("gx", "gy", None),
        P("gx", "gy", None),
        P("gx", "gy", None),
        P("gx", "gy", None, None),
        P("gx", "gy", None),
    )
    out_specs = (P("gx", "gy", None), P(("gx", "gy"), None))
    return jax.shard_map(
        per_device, mesh=mesh, in_specs=in_specs, out_specs=out_specs, check_vma=False
    )
```

```python
import functools

import jax
import jax.numpy as jnp
from jax import lax
from jax.experimental import pallas as pl
from jax.experimental.pallas import tpu as pltpu
from jax.sharding import PartitionSpec as P

STEPS = 3
TICKS = 2000
LATENT = 0.5
SHARE = 0.2
TICK_SHARE = SHARE / TICKS

HALO = 3
EDGE = 8
LEAD = 4
LANES = 128
TILE = 8
OFFSET = 2.0
FAR = 1e-30
CHUNKS = 8
OUTS = 4
UNROLL = 2
PUN = 2


def kelvin(h):
    return jnp.minimum(h, jnp.maximum(h - LATENT, 1.0 + OFFSET))


def face(one, two):
    return one[2] * two[2] * pl.reciprocal(one[1] + two[1], approx=True) * (two[0] - one[0])


def window_kernel(
    track, lateral, index_ref, h_hbm, k_hbm, bead_hbm, birth_hbm, xlo_ref, xhi_ref, ylo_ref, yhi_ref,
    clo_ref, chi_ref, out_hbm, rows_ref, h_v, k_v, bead_v, birth_v, hs, hn, ks, kz, bs, bz, ring_a,
    ring_b, acc_s, sem_in, sem_out,
):
    planes = track + 2 * HALO
    height = lateral + 2 * EDGE
    span = (lateral + 2 * LEAD) // TILE
    inner = pl.ds(EDGE, lateral)

    def copies(n):
        piece = track // CHUNKS
        src = pl.ds(n * piece, piece)
        dst = pl.ds(HALO + n * piece, piece)
        pairs = ((h_hbm, h_v), (k_hbm, k_v), (bead_hbm, bead_v), (birth_hbm, birth_v))
        return [
            pltpu.make_async_copy(hbm.at[src], vmem.at[dst, inner], sem_in.at[i, n])
            for i, (hbm, vmem) in enumerate(pairs)
        ]

    for n in range(CHUNKS):
        for copy in copies(n):
            copy.start()

    def place(h, k, birth, x, rows):
        inside = k > 0.0
        h_v[x, rows, :] = h
        bead_v[x, rows, :] = h
        k_v[x, rows, :] = jnp.where(inside, k, 1.0)
        birth_v[x, rows, :] = jnp.where(inside, birth, 1e6).astype(jnp.int32)

    for ref, first in ((xlo_ref, 0), (xhi_ref, HALO + track)):
        @pl.loop(0, HALO)
        def _(d, ref=ref, first=first):
            place(ref[d], ref[HALO + d], ref[2 * HALO + d], first + d, inner)
    for ref, first in ((ylo_ref, EDGE - HALO), (yhi_ref, EDGE + lateral)):
        @pl.loop(0, track)
        def _(x, ref=ref, first=first):
            place(ref[x, 0:HALO], ref[x, HALO:2 * HALO], ref[x, 2 * HALO:], x + HALO, pl.ds(first, HALO))
    for ref, first in ((clo_ref, 0), (chi_ref, HALO + track)):
        for d in range(HALO):
            for side, row in ((0, EDGE - HALO), (1, EDGE + lateral)):
                at = side * 3 * HALO
                place(
                    ref[d, at:at + HALO], ref[d, at + HALO:at + 2 * HALO], ref[d, at + 2 * HALO:at + 3 * HALO],
                    first + d, pl.ds(row, HALO),
                )

    top = lax.broadcasted_iota(jnp.int32, (TILE, LANES), 1) == LANES - 1

    def natural(j):
        return pl.ds(EDGE - LEAD + j, TILE, stride=span)

    def tile(j):
        return pl.ds(j * TILE, TILE)

    def prepare(x):
        for j in range(span):
            at, to = natural(j), tile(j)
            birth = birth_v[x, at, :]
            k = k_v[x, at, :]
            born = (birth >= 0) & (birth < STEPS * TICKS)
            b = birth.astype(jnp.float32) * TICK_SHARE
            hs[x, to, :] = jnp.where(born, bead_v[x, at, :], h_v[x, at, :]) + OFFSET
            ks[x, to, :] = k
            kz[x, to, :] = jnp.where(top, FAR, pltpu.roll(k, LANES - 1, 1))
            bs[x, to, :] = b
            bz[x, to, :] = pltpu.roll(b, LANES - 1, 1)

    def prepare_all(lo, hi):
        @pl.loop(0, (hi - lo) // PUN)
        def _(i):
            for u in range(PUN):
                prepare(lo + i * PUN + u)
        for x in range(hi - (hi - lo) % PUN, hi):
            prepare(x)

    prepare_all(0, HALO)
    prepare_all(HALO + track, planes)
    for n in range(CHUNKS):
        for copy in copies(n):
            copy.wait()
        piece = track // CHUNKS
        prepare_all(HALO + n * piece, HALO + (n + 1) * piece)

    def run_step(step, src, store, cuts):
        def share(b):
            return jnp.clip(SHARE * (step + 1) - b, 0.0, SHARE)

        def point(x, j):
            at = tile(j)
            h = src[x, at, :]
            t = kelvin(h)
            return h, (t, pl.reciprocal(ks[x, at, :] * t, approx=True), share(bs[x, at, :]))

        def put(ring, j, values):
            for ref, value in zip(ring, values):
                ref[tile(j), :] = value

        def get(ring, j):
            return [ref[tile(j), :] for ref in ring]

        for j in range(span):
            before = point(cuts[0] - 1, j)[1]
            h, now = point(cuts[0], j)
            put(ring_a, j, now)
            acc_s[tile(j), :] = h - face(before, now)

        def plane(x, here, there):
            cur = get(here, 0)
            beyond = [pltpu.roll(v, TILE - 1, 0) for v in cur]
            fy_old = pltpu.roll(face(get(here, span - 1), beyond), 1, 0)
            for j in range(span):
                at = tile(j)
                ahead = get(here, j + 1) if j + 1 < span else beyond
                h, nxt = point(x + 1, j)
                put(there, j, nxt)
                fx = face(cur, nxt)
                total = acc_s[at, :] + fx
                acc_s[at, :] = h - fx
                fy = face(cur, ahead)
                t = pltpu.roll(cur[0], LANES - 1, 1)
                fz = face(cur, (t, pl.reciprocal(kz[x, at, :] * t, approx=True), share(bz[x, at, :])))
                total = total + ((fy - fy_old) + (fz - pltpu.roll(fz, 1, 1)))
                store(x, j, total)
                cur, fy_old = ahead, fy

        for n, (lo, hi) in enumerate(zip(cuts[:-1], cuts[1:])):
            unroll = [u for u in (UNROLL, 2) if (hi - lo) % u == 0][0]

            @pl.loop(0, (hi - lo) // unroll)
            def _(i):
                for u in range(unroll):
                    rings = (ring_a, ring_b) if u % 2 == 0 else (ring_b, ring_a)
                    plane(lo + unroll * i + u, *rings)

            if step == STEPS - 1:
                out_copy(n).start()

    def out_copy(n):
        piece = track // OUTS
        return pltpu.make_async_copy(
            h_v.at[pl.ds(HALO + n * piece, piece), inner], out_hbm.at[pl.ds(n * piece, piece)], sem_out.at[n]
        )

    def into(ref):
        def store(x, j, value):
            ref[x, tile(j), :] = value
        return store

    def finish(x, j, value):
        h_v[x, natural(j), :] = value - OFFSET

    run_step(0, hs, into(hn), (1, planes - 1))
    run_step(1, hn, into(hs), (2, planes - 2))
    run_step(2, hs, finish, [HALO + n * (track // OUTS) for n in range(OUTS + 1)])

    h_v[0, 0:EDGE, :] = jnp.zeros((EDGE, LANES), jnp.float32)
    owners, slots = index_ref.shape
    flat = h_v.reshape(planes * height, LANES)

    @pl.loop(0, owners)
    def _(o):
        for k in range(slots):
            h = flat[pl.ds(index_ref[o, k], 1), :]
            rows_ref[pl.ds(o * slots + k, 1), :] = jnp.minimum(h, jnp.maximum(h - LATENT, 1.0))

    for n in range(OUTS):
        out_copy(n).wait()


def window(index, h, k, bead, birth, halos):
    track, lateral, stack = h.shape
    planes, height = track + 2 * HALO, lateral + 2 * EDGE
    owners, slots = index.shape
    anyspace = pl.BlockSpec(memory_space=pl.ANY)
    vmem = pl.BlockSpec(memory_space=pltpu.VMEM)
    grid_shape = (planes, height, stack)
    tiles_shape = (planes, lateral + 2 * LEAD, stack)
    return pl.pallas_call(
        functools.partial(window_kernel, track, lateral),
        out_shape=(
            jax.ShapeDtypeStruct(h.shape, jnp.float32),
            jax.ShapeDtypeStruct((owners * slots, stack), jnp.float32),
        ),
        in_specs=[pl.BlockSpec(memory_space=pltpu.SMEM)] + [anyspace] * 4 + [vmem] * 6,
        out_specs=(anyspace, vmem),
        scratch_shapes=[
            pltpu.VMEM(grid_shape, jnp.float32),
            pltpu.VMEM(grid_shape, jnp.float32),
            pltpu.VMEM(grid_shape, jnp.float32),
            pltpu.VMEM(grid_shape, jnp.int32),
            pltpu.VMEM(tiles_shape, jnp.float32),
            pltpu.VMEM(tiles_shape, jnp.float32),
            pltpu.VMEM(tiles_shape, jnp.float32),
            pltpu.VMEM(tiles_shape, jnp.float32),
            pltpu.VMEM(tiles_shape, jnp.float32),
            pltpu.VMEM(tiles_shape, jnp.float32),
            [pltpu.VMEM(tiles_shape[1:], jnp.float32)] * 3,
            [pltpu.VMEM(tiles_shape[1:], jnp.float32)] * 3,
            pltpu.VMEM(tiles_shape[1:], jnp.float32),
            pltpu.SemaphoreType.DMA((4, CHUNKS)),
            pltpu.SemaphoreType.DMA((OUTS,)),
        ],
        compiler_params=pltpu.CompilerParams(vmem_limit_bytes=58 * 1024 * 1024),
    )(index, h, k, bead, birth, *halos)


def shift(axis, by):
    count = lax.axis_size(axis)
    return [(i, i + by) for i in range(count) if 0 <= i + by < count]


def per_device(enthalpy, conductivity, bead_enthalpy, birth_time, send_rows, send_counts):
    track, lateral, _ = enthalpy.shape

    def fields(cut):
        birth = birth_time[cut]
        born = (birth >= 0) & (birth < STEPS * TICKS)
        return (
            jnp.where(born, bead_enthalpy[cut], enthalpy[cut]),
            conductivity[cut],
            birth.astype(jnp.float32),
        )

    low, high = slice(0, HALO), slice(-HALO, None)
    xlo = lax.ppermute(jnp.concatenate(fields((high,)), 0), "gx", shift("gx", 1))
    xhi = lax.ppermute(jnp.concatenate(fields((low,)), 0), "gx", shift("gx", -1))
    ylo = lax.ppermute(jnp.concatenate(fields((slice(None), high)), 1), "gy", shift("gy", 1))
    yhi = lax.ppermute(jnp.concatenate(fields((slice(None), low)), 1), "gy", shift("gy", -1))
    clo = lax.ppermute(jnp.concatenate([ylo[-HALO:], yhi[-HALO:]], 1), "gx", shift("gx", 1))
    chi = lax.ppermute(jnp.concatenate([ylo[:HALO], yhi[:HALO]], 1), "gx", shift("gx", -1))

    rows, counts = send_rows[0, 0], send_counts[0, 0]
    slot = jnp.arange(rows.shape[1], dtype=jnp.int32)
    place = (rows // lateral + HALO) * (lateral + 2 * EDGE) + rows % lateral + EDGE
    index = jnp.where(slot[None, :] < counts[:, None], place, 0)
    end, outgoing = window(
        index, enthalpy, conductivity, bead_enthalpy, birth_time, (xlo, xhi, ylo, yhi, clo, chi)
    )
    outgoing = outgoing.reshape(rows.shape + outgoing.shape[1:])
    received = lax.all_to_all(outgoing, ("gx", "gy"), split_axis=0, concat_axis=0, tiled=True)
    return end, received.reshape(-1, received.shape[-1])


def solution(mesh):
    in_specs = (
        P("gx", "gy", None),
        P("gx", "gy", None),
        P("gx", "gy", None),
        P("gx", "gy", None),
        P("gx", "gy", None, None),
        P("gx", "gy", None),
    )
    out_specs = (P("gx", "gy", None), P(("gx", "gy"), None))
    return jax.shard_map(
        per_device, mesh=mesh, in_specs=in_specs, out_specs=out_specs, check_vma=False
    )
```

```python
import functools

import jax
import jax.numpy as jnp
from jax import lax
from jax.experimental import pallas as pl
from jax.experimental.pallas import tpu as pltpu
from jax.sharding import PartitionSpec as P

STEPS = 3
TICKS = 2000
LATENT = 0.5
SHARE = 0.2
TICK_SHARE = SHARE / TICKS

HALO = 3
EDGE = 8
LEAD = 4
LANES = 128
TILE = 8
OFFSET = 2.0
FAR = 1e-30
CHUNKS = 8
OUTS = 4
UNROLL = 4
PUN = 2
RIM = 3 * HALO
MIB = 1024 * 1024

ANY = pl.BlockSpec(memory_space=pl.ANY)
VMEM = pl.BlockSpec(memory_space=pltpu.VMEM)
SMEM = pl.BlockSpec(memory_space=pltpu.SMEM)


def kelvin(h):
    return jnp.minimum(h, jnp.maximum(h - LATENT, 1.0))


def lifted_kelvin(h):
    return jnp.minimum(h, jnp.maximum(h - LATENT, 1.0 + OFFSET))


def standing(h, bead, birth):
    return jnp.where((birth >= 0) & (birth < STEPS * TICKS), bead, h)


def face(one, two):
    return one[2] * two[2] * pl.reciprocal(one[1] + two[1], approx=True) * (two[0] - one[0])


def tile(j):
    return pl.ds(j * TILE, TILE)


class Slab:
    def __init__(self, raw, grids, rings, acc):
        self.raw = raw
        self.ha, self.hb, self.ks, self.kz, self.bs, self.bz = grids
        self.rings = rings
        self.acc = acc
        self.height = raw[0].shape[1]
        self.span = (self.height - 2 * (EDGE - LEAD)) // TILE

    def natural(self, j):
        return pl.ds(EDGE - LEAD + j, TILE, stride=self.span)

    def place(self, h, k, birth, x, rows):
        inside = k > 0.0
        values = (h, jnp.where(inside, k, 1.0), h, jnp.where(inside, birth, 1e6).astype(jnp.int32))
        for ref, value in zip(self.raw, values):
            ref[x, rows, :] = value

    def prepare(self, x):
        h_v, k_v, bead_v, birth_v = self.raw
        top = lax.broadcasted_iota(jnp.int32, (TILE, LANES), 1) == LANES - 1
        for j in range(self.span):
            at, to = self.natural(j), tile(j)
            birth, k = birth_v[x, at, :], k_v[x, at, :]
            b = birth.astype(jnp.float32) * TICK_SHARE
            self.ha[x, to, :] = standing(h_v[x, at, :], bead_v[x, at, :], birth) + OFFSET
            self.ks[x, to, :] = k
            self.kz[x, to, :] = jnp.where(top, FAR, pltpu.roll(k, LANES - 1, 1))
            self.bs[x, to, :] = b
            self.bz[x, to, :] = pltpu.roll(b, LANES - 1, 1)

    def prepare_all(self, lo, hi):
        @pl.loop(0, (hi - lo) // PUN)
        def _(i):
            for u in range(PUN):
                self.prepare(lo + i * PUN + u)

    def into(self, ref):
        def store(x, j, value):
            ref[x, tile(j), :] = value
        return store

    def run_step(self, step, src, store, base, cuts, after=None):
        span, acc, (ring_a, ring_b) = self.span, self.acc, self.rings

        def share(b):
            return jnp.clip(SHARE * (step + 1) - b, 0.0, SHARE)

        def point(x, j):
            at = tile(j)
            h = src[x, at, :]
            t = lifted_kelvin(h)
            return h, (t, pl.reciprocal(self.ks[x, at, :] * t, approx=True), share(self.bs[x, at, :]))

        def put(ring, j, values):
            for ref, value in zip(ring, values):
                ref[tile(j), :] = value

        def get(ring, j):
            return [ref[tile(j), :] for ref in ring]

        for j in range(span):
            before = point(base + cuts[0] - 1, j)[1]
            h, now = point(base + cuts[0], j)
            put(ring_a, j, now)
            acc[tile(j), :] = h - face(before, now)

        def plane(x, here, there):
            cur = get(here, 0)
            beyond = [pltpu.roll(v, TILE - 1, 0) for v in cur]
            fy_old = pltpu.roll(face(get(here, span - 1), beyond), 1, 0)
            for j in range(span):
                at = tile(j)
                ahead = get(here, j + 1) if j + 1 < span else beyond
                h, nxt = point(x + 1, j)
                put(there, j, nxt)
                fx = face(cur, nxt)
                total = acc[at, :] + fx
                acc[at, :] = h - fx
                fy = face(cur, ahead)
                t = pltpu.roll(cur[0], LANES - 1, 1)
                fz = face(
                    cur, (t, pl.reciprocal(self.kz[x, at, :] * t, approx=True), share(self.bz[x, at, :]))
                )
                store(x, j, total + ((fy - fy_old) + (fz - pltpu.roll(fz, 1, 1))))
                cur, fy_old = ahead, fy

        for n, (lo, hi) in enumerate(zip(cuts[:-1], cuts[1:])):
            unroll = UNROLL if (hi - lo) % UNROLL == 0 else 2

            @pl.loop(0, (hi - lo) // unroll)
            def _(i):
                for u in range(unroll):
                    rings = (ring_a, ring_b) if u % 2 == 0 else (ring_b, ring_a)
                    plane(base + lo + unroll * i + u, *rings)

            if (hi - lo) % 2:
                plane(base + hi - 1, ring_a, ring_b)
            if after is not None:
                after(n)


def slab_scratch(planes, lateral, stack):
    tiles = (lateral + 2 * LEAD, stack)
    raw = (planes, lateral + 2 * EDGE, stack)
    return [
        [pltpu.VMEM(raw, dtype) for dtype in (jnp.float32, jnp.float32, jnp.float32, jnp.int32)],
        [pltpu.VMEM((planes,) + tiles, jnp.float32)] * 6,
        [[pltpu.VMEM(tiles, jnp.float32)] * 3] * 2,
        pltpu.VMEM(tiles, jnp.float32),
    ]


def strip_kernel(
    h_hbm, k_hbm, bead_hbm, birth_hbm, xlo_ref, xhi_ref, ylo_ref, yhi_ref, xs, ys, sem
):
    track, lateral, _ = h_hbm.shape
    copies = []
    for i, hbm in enumerate((h_hbm, k_hbm, bead_hbm, birth_hbm)):
        for side in range(2):
            planes = pl.ds(side * (track - HALO), HALO)
            rows = pl.ds(side * (lateral - EDGE), EDGE)
            copies.append(pltpu.make_async_copy(hbm.at[planes], xs[i].at[side], sem.at[0, i, side]))
            copies.append(pltpu.make_async_copy(hbm.at[:, rows], ys[i].at[side], sem.at[1, i, side]))
    for copy in copies:
        copy.start()
    for copy in copies:
        copy.wait()
    for side, out in ((0, xlo_ref), (1, xhi_ref)):
        @pl.loop(0, HALO)
        def _(d, side=side, out=out):
            birth = xs[3][side, d]
            out[d] = standing(xs[0][side, d], xs[2][side, d], birth)
            out[HALO + d] = xs[1][side, d]
            out[2 * HALO + d] = birth.astype(jnp.float32)
    flat = [ref.reshape(2 * track * EDGE, LANES) for ref in ys]
    for side, out in ((0, ylo_ref), (1, yhi_ref)):
        for i in range(track // TILE):
            for d in range(HALO):
                row = (side * track + i * TILE) * EDGE + d + side * (EDGE - HALO)
                h, k, bead, birth = [ref[pl.ds(row, TILE, stride=EDGE), :] for ref in flat]
                out[d, tile(i), :] = standing(h, bead, birth)
                out[HALO + d, tile(i), :] = k
                out[2 * HALO + d, tile(i), :] = birth.astype(jnp.float32)


def strips(h, k, bead, birth):
    track, lateral, stack = h.shape
    types = (jnp.float32, jnp.float32, jnp.float32, jnp.int32)
    return pl.pallas_call(
        strip_kernel,
        out_shape=(
            jax.ShapeDtypeStruct((3 * HALO, lateral, stack), jnp.float32),
            jax.ShapeDtypeStruct((3 * HALO, lateral, stack), jnp.float32),
            jax.ShapeDtypeStruct((3 * HALO, track, stack), jnp.float32),
            jax.ShapeDtypeStruct((3 * HALO, track, stack), jnp.float32),
        ),
        in_specs=[ANY] * 4,
        out_specs=(VMEM,) * 4,
        scratch_shapes=[
            [pltpu.VMEM((2, HALO, lateral, stack), dtype) for dtype in types],
            [pltpu.VMEM((2, track, EDGE, stack), dtype) for dtype in types],
            pltpu.SemaphoreType.DMA((2, 4, 2)),
        ],
        compiler_params=pltpu.CompilerParams(vmem_limit_bytes=16 * MIB),
    )(h, k, bead, birth)


def inner_kernel(
    h_hbm, k_hbm, bead_hbm, birth_hbm, ylo_ref, yhi_ref, out_hbm, raw, grids, rings, acc, sem_in, sem_out
):
    track, lateral, _ = h_hbm.shape
    slab = Slab(raw, grids, rings, acc)
    inner = pl.ds(EDGE, lateral)
    piece = track // CHUNKS

    def copies(n):
        at = pl.ds(n * piece, piece)
        return [
            pltpu.make_async_copy(hbm.at[at], vmem.at[at, inner], sem_in.at[i, n])
            for i, (hbm, vmem) in enumerate(zip((h_hbm, k_hbm, bead_hbm, birth_hbm), raw))
        ]

    for n in range(CHUNKS):
        for copy in copies(n):
            copy.start()

    height = lateral + 2 * EDGE
    flat = [ref.reshape(track * height, LANES) for ref in raw]
    for ref, first in ((ylo_ref, EDGE - HALO), (yhi_ref, EDGE + lateral)):
        @pl.loop(0, track // TILE)
        def _(i, ref=ref, first=first):
            for d in range(HALO):
                h, k, birth = [ref[f * HALO + d, pl.ds(i * TILE, TILE), :] for f in range(3)]
                at = pl.ds(i * TILE * height + first + d, TILE, stride=height)
                inside = k > 0.0
                flat[0][at, :] = h
                flat[1][at, :] = jnp.where(inside, k, 1.0)
                flat[2][at, :] = h
                flat[3][at, :] = jnp.where(inside, birth, 1e6).astype(jnp.int32)

    for n in range(CHUNKS):
        for copy in copies(n):
            copy.wait()
        slab.prepare_all(n * piece, (n + 1) * piece)

    cuts = [HALO] + [n * (track // OUTS) + HALO for n in range(1, OUTS)] + [track - HALO]

    def out_copy(n):
        at = pl.ds(cuts[n], cuts[n + 1] - cuts[n])
        return pltpu.make_async_copy(raw[0].at[at, inner], out_hbm.at[at], sem_out.at[n])

    def finish(x, j, value):
        raw[0][x, slab.natural(j), :] = value - OFFSET

    slab.run_step(0, slab.ha, slab.into(slab.hb), 0, (1, track - 1))
    slab.run_step(1, slab.hb, slab.into(slab.ha), 0, (2, track - 2))
    slab.run_step(2, slab.ha, finish, 0, cuts, lambda n: out_copy(n).start())
    for n in range(OUTS):
        out_copy(n).wait()


def inner_planes(h, k, bead, birth, ylo, yhi):
    track, lateral, stack = h.shape
    return pl.pallas_call(
        inner_kernel,
        out_shape=jax.ShapeDtypeStruct(h.shape, jnp.float32),
        in_specs=[ANY] * 4 + [VMEM] * 2,
        out_specs=ANY,
        scratch_shapes=slab_scratch(track, lateral, stack) + [
            pltpu.SemaphoreType.DMA((4, CHUNKS)),
            pltpu.SemaphoreType.DMA((OUTS,)),
        ],
        compiler_params=pltpu.CompilerParams(vmem_limit_bytes=52 * MIB),
        cost_estimate=pl.CostEstimate(
            flops=200 * h.size, bytes_accessed=20 * h.size, transcendentals=15 * h.size
        ),
    )(h, k, bead, birth, ylo, yhi)


def rim_kernel(
    index_ref, h_hbm, k_hbm, bead_hbm, birth_hbm, part_hbm, xlo_ref, xhi_ref, ylo_ref, yhi_ref, clo_ref,
    chi_ref, out_hbm, rows_ref, raw, grids, rings, acc, whole, sem_in, sem_part, sem_out,
):
    track, lateral, _ = h_hbm.shape
    slab = Slab(raw, grids, rings, acc)
    inner = pl.ds(EDGE, lateral)
    own = RIM - HALO

    copies = []
    for i, (hbm, vmem) in enumerate(zip((h_hbm, k_hbm, bead_hbm, birth_hbm), raw)):
        for side in range(2):
            src = pl.ds(side * (track - own), own)
            dst = pl.ds(HALO + side * own, own)
            copies.append(pltpu.make_async_copy(hbm.at[src], vmem.at[dst, inner], sem_in.at[i, side]))
    for copy in copies:
        copy.start()
    middle = pl.ds(HALO, track - 2 * HALO)
    part = pltpu.make_async_copy(part_hbm.at[middle], whole.at[middle, inner], sem_part)
    part.start()

    for side, ref in ((0, xlo_ref), (1, xhi_ref)):
        @pl.loop(0, HALO)
        def _(d, side=side, ref=ref):
            slab.place(ref[d], ref[HALO + d], ref[2 * HALO + d], side * (RIM + own) + d, inner)
    for x in range(2 * RIM):
        beyond = x < HALO or x >= HALO + 2 * own
        for y in range(2):
            if beyond:
                ref, plane, first = (clo_ref, chi_ref)[x >= HALO], x % RIM - (own if x >= HALO else 0), y * RIM
            else:
                ref, plane, first = (ylo_ref, yhi_ref)[y], x - HALO + (track - 2 * own if x >= RIM else 0), 0
            for d in range(HALO):
                h, k, birth = [ref[first + f * HALO + d, pl.ds(plane, 1), :] for f in range(3)]
                slab.place(h, k, birth, x, pl.ds((EDGE - HALO, EDGE + lateral)[y] + d, 1))

    for copy in copies:
        copy.wait()
    slab.prepare_all(0, 2 * RIM)

    def finish(x, j, value):
        at = x - HALO + jnp.where(x >= RIM, track - 2 * own, 0)
        whole[at, slab.natural(j), :] = value - OFFSET

    @pl.loop(0, 2)
    def _(side):
        base = side * RIM
        slab.run_step(0, slab.ha, slab.into(slab.hb), base, (1, RIM - 1))
        slab.run_step(1, slab.hb, slab.into(slab.ha), base, (2, RIM - 2))
        slab.run_step(2, slab.ha, finish, base, (3, RIM - 3))

    outs = []
    for side in range(2):
        at = pl.ds(side * (track - HALO), HALO)
        outs.append(pltpu.make_async_copy(whole.at[at, inner], out_hbm.at[at], sem_out.at[side]))
    for copy in outs:
        copy.start()
    part.wait()

    whole[0, 0:EDGE, :] = jnp.zeros((EDGE, LANES), jnp.float32)
    owners, slots = index_ref.shape
    flat = whole.reshape(track * (lateral + 2 * EDGE), LANES)

    @pl.loop(0, owners)
    def _(o):
        for k in range(slots):
            rows_ref[pl.ds(o * slots + k, 1), :] = kelvin(flat[pl.ds(index_ref[o, k], 1), :])

    for copy in outs:
        copy.wait()


def rim_and_rows(index, h, k, bead, birth, part, halos):
    track, lateral, stack = h.shape
    owners, slots = index.shape
    return pl.pallas_call(
        rim_kernel,
        out_shape=(
            jax.ShapeDtypeStruct(h.shape, jnp.float32),
            jax.ShapeDtypeStruct((owners * slots, stack), jnp.float32),
        ),
        in_specs=[SMEM] + [ANY] * 5 + [VMEM] * 6,
        out_specs=(ANY, VMEM),
        input_output_aliases={5: 0},
        scratch_shapes=slab_scratch(2 * RIM, lateral, stack) + [
            pltpu.VMEM((track, lateral + 2 * EDGE, stack), jnp.float32),
            pltpu.SemaphoreType.DMA((4, 2)),
            pltpu.SemaphoreType.DMA,
            pltpu.SemaphoreType.DMA((2,)),
        ],
        compiler_params=pltpu.CompilerParams(vmem_limit_bytes=32 * MIB),
        cost_estimate=pl.CostEstimate(
            flops=50 * h.size, bytes_accessed=6 * h.size, transcendentals=4 * h.size
        ),
    )(index, h, k, bead, birth, part, *halos)


def shift(axis, by):
    count = lax.axis_size(axis)
    return [(i, i + by) for i in range(count) if 0 <= i + by < count]


def per_device(enthalpy, conductivity, bead_enthalpy, birth_time, send_rows, send_counts):
    lateral = enthalpy.shape[1]
    fields = (enthalpy, conductivity, bead_enthalpy, birth_time)

    to_low, to_high, to_left, to_right = strips(*fields)
    ylo = lax.ppermute(to_right, "gy", shift("gy", 1))
    yhi = lax.ppermute(to_left, "gy", shift("gy", -1))
    xlo = lax.ppermute(to_high, "gx", shift("gx", 1))
    xhi = lax.ppermute(to_low, "gx", shift("gx", -1))
    clo = lax.ppermute(jnp.concatenate([ylo[:, -HALO:], yhi[:, -HALO:]], 0), "gx", shift("gx", 1))
    chi = lax.ppermute(jnp.concatenate([ylo[:, :HALO], yhi[:, :HALO]], 0), "gx", shift("gx", -1))

    rows, counts = send_rows[0, 0], send_counts[0, 0]
    slot = jnp.arange(rows.shape[1], dtype=jnp.int32)
    place = rows // lateral * (lateral + 2 * EDGE) + rows % lateral + EDGE
    index = jnp.where(slot[None, :] < counts[:, None], place, 0)

    part = inner_planes(*fields, ylo, yhi)
    end, outgoing = rim_and_rows(index, *fields, part, (xlo, xhi, ylo, yhi, clo, chi))
    outgoing = outgoing.reshape(rows.shape + outgoing.shape[1:])
    received = lax.all_to_all(outgoing, ("gx", "gy"), split_axis=0, concat_axis=0, tiled=True)
    return end, received.reshape(-1, received.shape[-1])


def solution(mesh):
    in_specs = (
        P("gx", "gy", None),
        P("gx", "gy", None),
        P("gx", "gy", None),
        P("gx", "gy", None),
        P("gx", "gy", None, None),
        P("gx", "gy", None),
    )
    out_specs = (P("gx", "gy", None), P(("gx", "gy"), None))
    return jax.shard_map(
        per_device, mesh=mesh, in_specs=in_specs, out_specs=out_specs, check_vma=False
    )
```

```python
import functools

import jax
import jax.numpy as jnp
from jax import lax
from jax.experimental import pallas as pl
from jax.experimental.pallas import tpu as pltpu
from jax.sharding import PartitionSpec as P

STEPS = 3
TICKS = 2000
LATENT = 0.5
SHARE = 0.2
TICK_SHARE = SHARE / TICKS

HALO = 3
EDGE = 8
LEAD = 4
LANES = 128
TILE = 8
OFFSET = 2.0
FAR = 1e-30
CHUNKS = 8
OUTS = 4
UNROLL = 4
PUN = 2
RIM = 3 * HALO
MIB = 1024 * 1024
VMEM_ALL = 60 * MIB

ANY = pl.BlockSpec(memory_space=pl.ANY)
VMEM = pl.BlockSpec(memory_space=pltpu.VMEM)
SMEM = pl.BlockSpec(memory_space=pltpu.SMEM)


def kelvin(h):
    return jnp.minimum(h, jnp.maximum(h - LATENT, 1.0))


def lifted_kelvin(h):
    return jnp.minimum(h, jnp.maximum(h - LATENT, 1.0 + OFFSET))


def standing(h, bead, birth):
    return jnp.where((birth >= 0) & (birth < STEPS * TICKS), bead, h)


def face(one, two):
    return one[2] * two[2] * pl.reciprocal(one[1] + two[1], approx=True) * (two[0] - one[0])


def tile(j):
    return pl.ds(j * TILE, TILE)


class Slab:
    def __init__(self, raw, grids, rings, acc):
        self.raw = raw
        self.ha, self.hb, self.ks, self.kz, self.bs, self.bz = grids
        self.rings = rings
        self.acc = acc
        self.height = raw[0].shape[1]
        self.span = (self.height - 2 * (EDGE - LEAD)) // TILE

    def natural(self, j):
        return pl.ds(EDGE - LEAD + j, TILE, stride=self.span)

    def place(self, h, k, birth, x, rows):
        inside = k > 0.0
        values = (h, jnp.where(inside, k, 1.0), h, jnp.where(inside, birth, 1e6).astype(jnp.int32))
        for ref, value in zip(self.raw, values):
            ref[x, rows, :] = value

    def prepare(self, x):
        h_v, k_v, bead_v, birth_v = self.raw
        top = lax.broadcasted_iota(jnp.int32, (TILE, LANES), 1) == LANES - 1
        for j in range(self.span):
            at, to = self.natural(j), tile(j)
            birth, k = birth_v[x, at, :], k_v[x, at, :]
            b = birth.astype(jnp.float32) * TICK_SHARE
            self.ha[x, to, :] = standing(h_v[x, at, :], bead_v[x, at, :], birth) + OFFSET
            self.ks[x, to, :] = k
            self.kz[x, to, :] = jnp.where(top, FAR, pltpu.roll(k, LANES - 1, 1))
            self.bs[x, to, :] = b
            self.bz[x, to, :] = pltpu.roll(b, LANES - 1, 1)

    def prepare_all(self, lo, hi):
        @pl.loop(0, (hi - lo) // PUN)
        def _(i):
            for u in range(PUN):
                self.prepare(lo + i * PUN + u)

    def into(self, ref):
        def store(x, j, value):
            ref[x, tile(j), :] = value
        return store

    def run_step(self, step, src, store, base, cuts, after=None):
        span, acc, (ring_a, ring_b) = self.span, self.acc, self.rings

        def share(b):
            return jnp.clip(SHARE * (step + 1) - b, 0.0, SHARE)

        def point(x, j):
            at = tile(j)
            h = src[x, at, :]
            t = lifted_kelvin(h)
            return h, (t, pl.reciprocal(self.ks[x, at, :] * t, approx=True), share(self.bs[x, at, :]))

        def put(ring, j, values):
            for ref, value in zip(ring, values):
                ref[tile(j), :] = value

        def get(ring, j):
            return [ref[tile(j), :] for ref in ring]

        for j in range(span):
            before = point(base + cuts[0] - 1, j)[1]
            h, now = point(base + cuts[0], j)
            put(ring_a, j, now)
            acc[tile(j), :] = h - face(before, now)

        def plane(x, here, there):
            cur = get(here, 0)
            beyond = [pltpu.roll(v, TILE - 1, 0) for v in cur]
            fy_old = pltpu.roll(face(get(here, span - 1), beyond), 1, 0)
            for j in range(span):
                at = tile(j)
                ahead = get(here, j + 1) if j + 1 < span else beyond
                h, nxt = point(x + 1, j)
                put(there, j, nxt)
                fx = face(cur, nxt)
                total = acc[at, :] + fx
                acc[at, :] = h - fx
                fy = face(cur, ahead)
                t = pltpu.roll(cur[0], LANES - 1, 1)
                fz = face(
                    cur, (t, pl.reciprocal(self.kz[x, at, :] * t, approx=True), share(self.bz[x, at, :]))
                )
                store(x, j, total + ((fy - fy_old) + (fz - pltpu.roll(fz, 1, 1))))
                cur, fy_old = ahead, fy

        for n, (lo, hi) in enumerate(zip(cuts[:-1], cuts[1:])):
            unroll = UNROLL if (hi - lo) % UNROLL == 0 else 2

            @pl.loop(0, (hi - lo) // unroll)
            def _(i):
                for u in range(unroll):
                    rings = (ring_a, ring_b) if u % 2 == 0 else (ring_b, ring_a)
                    plane(base + lo + unroll * i + u, *rings)

            if (hi - lo) % 2:
                plane(base + hi - 1, ring_a, ring_b)
            if after is not None:
                after(n)


def slab_scratch(planes, lateral, stack):
    tiles = (lateral + 2 * LEAD, stack)
    raw = (planes, lateral + 2 * EDGE, stack)
    return [
        [pltpu.VMEM(raw, dtype) for dtype in (jnp.float32, jnp.float32, jnp.float32, jnp.int32)],
        [pltpu.VMEM((planes,) + tiles, jnp.float32)] * 6,
        [[pltpu.VMEM(tiles, jnp.float32)] * 3] * 2,
        pltpu.VMEM(tiles, jnp.float32),
    ]


def strip_kernel(
    h_hbm, k_hbm, bead_hbm, birth_hbm, xlo_ref, xhi_ref, ylo_ref, yhi_ref, xs, ys, sem
):
    track, lateral, _ = h_hbm.shape
    copies = []
    for i, hbm in enumerate((h_hbm, k_hbm, bead_hbm, birth_hbm)):
        for side in range(2):
            planes = pl.ds(side * (track - HALO), HALO)
            rows = pl.ds(side * (lateral - EDGE), EDGE)
            copies.append(pltpu.make_async_copy(hbm.at[planes], xs[i].at[side], sem.at[0, i, side]))
            copies.append(pltpu.make_async_copy(hbm.at[:, rows], ys[i].at[side], sem.at[1, i, side]))
    for copy in copies:
        copy.start()
    for copy in copies:
        copy.wait()
    for side, out in ((0, xlo_ref), (1, xhi_ref)):
        @pl.loop(0, HALO)
        def _(d, side=side, out=out):
            birth = xs[3][side, d]
            rows = pl.ds(0, lateral)
            out[d, rows, :] = standing(xs[0][side, d], xs[2][side, d], birth)
            out[HALO + d, rows, :] = xs[1][side, d]
            out[2 * HALO + d, rows, :] = birth.astype(jnp.float32)
    flat = [ref.reshape(2 * track * EDGE, LANES) for ref in ys]
    for side, out in ((0, ylo_ref), (1, yhi_ref)):
        for i in range(track // TILE):
            for d in range(HALO):
                row = (side * track + i * TILE) * EDGE + d + side * (EDGE - HALO)
                h, k, bead, birth = [ref[pl.ds(row, TILE, stride=EDGE), :] for ref in flat]
                out[d, tile(i), :] = standing(h, bead, birth)
                out[HALO + d, tile(i), :] = k
                out[2 * HALO + d, tile(i), :] = birth.astype(jnp.float32)


def strips(h, k, bead, birth):
    track, lateral, stack = h.shape
    types = (jnp.float32, jnp.float32, jnp.float32, jnp.int32)
    return pl.pallas_call(
        strip_kernel,
        out_shape=(
            jax.ShapeDtypeStruct((3 * HALO, lateral + EDGE, stack), jnp.float32),
            jax.ShapeDtypeStruct((3 * HALO, lateral + EDGE, stack), jnp.float32),
            jax.ShapeDtypeStruct((3 * HALO, track, stack), jnp.float32),
            jax.ShapeDtypeStruct((3 * HALO, track, stack), jnp.float32),
        ),
        in_specs=[ANY] * 4,
        out_specs=(VMEM,) * 4,
        scratch_shapes=[
            [pltpu.VMEM((2, HALO, lateral, stack), dtype) for dtype in types],
            [pltpu.VMEM((2, track, EDGE, stack), dtype) for dtype in types],
            pltpu.SemaphoreType.DMA((2, 4, 2)),
        ],
        compiler_params=pltpu.CompilerParams(vmem_limit_bytes=VMEM_ALL),
    )(h, k, bead, birth)


def inner_kernel(
    h_hbm, k_hbm, bead_hbm, birth_hbm, ylo_ref, yhi_ref, out_hbm, raw, grids, rings, acc, sem_in, sem_out
):
    track, lateral, _ = h_hbm.shape
    slab = Slab(raw, grids, rings, acc)
    inner = pl.ds(EDGE, lateral)
    piece = track // CHUNKS

    def copies(n):
        at = pl.ds(n * piece, piece)
        return [
            pltpu.make_async_copy(hbm.at[at], vmem.at[at, inner], sem_in.at[i, n])
            for i, (hbm, vmem) in enumerate(zip((h_hbm, k_hbm, bead_hbm, birth_hbm), raw))
        ]

    for n in range(CHUNKS):
        for copy in copies(n):
            copy.start()

    height = lateral + 2 * EDGE
    flat = [ref.reshape(track * height, LANES) for ref in raw]
    for ref, first in ((ylo_ref, EDGE - HALO), (yhi_ref, EDGE + lateral)):
        @pl.loop(0, track // TILE)
        def _(i, ref=ref, first=first):
            for d in range(HALO):
                h, k, birth = [ref[f * HALO + d, pl.ds(i * TILE, TILE), :] for f in range(3)]
                at = pl.ds(i * TILE * height + first + d, TILE, stride=height)
                inside = k > 0.0
                flat[0][at, :] = h
                flat[1][at, :] = jnp.where(inside, k, 1.0)
                flat[2][at, :] = h
                flat[3][at, :] = jnp.where(inside, birth, 1e6).astype(jnp.int32)

    for n in range(CHUNKS):
        for copy in copies(n):
            copy.wait()
        slab.prepare_all(n * piece, (n + 1) * piece)

    cuts = [HALO] + [n * (track // OUTS) + HALO for n in range(1, OUTS)] + [track - HALO]

    def out_copy(n):
        at = pl.ds(cuts[n], cuts[n + 1] - cuts[n])
        return pltpu.make_async_copy(raw[0].at[at, inner], out_hbm.at[at], sem_out.at[n])

    def finish(x, j, value):
        raw[0][x, slab.natural(j), :] = value - OFFSET

    slab.run_step(0, slab.ha, slab.into(slab.hb), 0, (1, track - 1))
    slab.run_step(1, slab.hb, slab.into(slab.ha), 0, (2, track - 2))
    slab.run_step(2, slab.ha, finish, 0, cuts, lambda n: out_copy(n).start())
    for n in range(OUTS):
        out_copy(n).wait()


def inner_planes(h, k, bead, birth, ylo, yhi):
    track, lateral, stack = h.shape
    return pl.pallas_call(
        inner_kernel,
        out_shape=jax.ShapeDtypeStruct(h.shape, jnp.float32),
        in_specs=[ANY] * 4 + [VMEM] * 2,
        out_specs=ANY,
        scratch_shapes=slab_scratch(track, lateral, stack) + [
            pltpu.SemaphoreType.DMA((4, CHUNKS)),
            pltpu.SemaphoreType.DMA((OUTS,)),
        ],
        compiler_params=pltpu.CompilerParams(vmem_limit_bytes=58 * MIB),
        cost_estimate=pl.CostEstimate(
            flops=200 * h.size, bytes_accessed=20 * h.size, transcendentals=15 * h.size
        ),
    )(h, k, bead, birth, ylo, yhi)


def rim_kernel(
    index_ref, h_hbm, k_hbm, bead_hbm, birth_hbm, part_hbm, xlo_ref, xhi_ref, ylo_ref, yhi_ref,
    out_hbm, rows_ref, raw, grids, rings, acc, whole, sem_in, sem_part, sem_out,
):
    track, lateral, _ = h_hbm.shape
    slab = Slab(raw, grids, rings, acc)
    inner = pl.ds(EDGE, lateral)
    own = RIM - HALO

    copies = []
    for i, (hbm, vmem) in enumerate(zip((h_hbm, k_hbm, bead_hbm, birth_hbm), raw)):
        for side in range(2):
            src = pl.ds(side * (track - own), own)
            dst = pl.ds(HALO + side * own, own)
            copies.append(pltpu.make_async_copy(hbm.at[src], vmem.at[dst, inner], sem_in.at[i, side]))
    for copy in copies:
        copy.start()
    middle = pl.ds(HALO, track - 2 * HALO)
    part = pltpu.make_async_copy(part_hbm.at[middle], whole.at[middle, inner], sem_part)
    part.start()

    below, above = pl.ds(EDGE - HALO, HALO), pl.ds(EDGE + lateral, HALO)
    for side, ref in ((0, xlo_ref), (1, xhi_ref)):
        @pl.loop(0, HALO)
        def _(d, side=side, ref=ref):
            for first, n, rows in ((0, lateral, inner), (lateral, HALO, below), (lateral + HALO, HALO, above)):
                slab.place(
                    *[ref[f * HALO + d, pl.ds(first, n), :] for f in range(3)], side * (RIM + own) + d, rows
                )
    for x in range(HALO, HALO + 2 * own):
        at = pl.ds(x - HALO + (track - 2 * own if x >= RIM else 0), 1)
        for y, ref in enumerate((ylo_ref, yhi_ref)):
            for d in range(HALO):
                row = pl.ds((EDGE - HALO, EDGE + lateral)[y] + d, 1)
                slab.place(*[ref[f * HALO + d, at, :] for f in range(3)], x, row)

    for copy in copies:
        copy.wait()
    slab.prepare_all(0, 2 * RIM)

    def finish(x, j, value):
        at = x - HALO + jnp.where(x >= RIM, track - 2 * own, 0)
        whole[at, slab.natural(j), :] = value - OFFSET

    @pl.loop(0, 2)
    def _(side):
        base = side * RIM
        slab.run_step(0, slab.ha, slab.into(slab.hb), base, (1, RIM - 1))
        slab.run_step(1, slab.hb, slab.into(slab.ha), base, (2, RIM - 2))
        slab.run_step(2, slab.ha, finish, base, (3, RIM - 3))

    outs = []
    for side in range(2):
        at = pl.ds(side * (track - HALO), HALO)
        outs.append(pltpu.make_async_copy(whole.at[at, inner], out_hbm.at[at], sem_out.at[side]))
    for copy in outs:
        copy.start()
    part.wait()

    whole[0, 0:EDGE, :] = jnp.zeros((EDGE, LANES), jnp.float32)
    owners, slots = index_ref.shape
    flat = whole.reshape(track * (lateral + 2 * EDGE), LANES)

    @pl.loop(0, owners)
    def _(o):
        for k in range(slots):
            rows_ref[pl.ds(o * slots + k, 1), :] = kelvin(flat[pl.ds(index_ref[o, k], 1), :])

    for copy in outs:
        copy.wait()


def rim_and_rows(index, h, k, bead, birth, part, halos):
    track, lateral, stack = h.shape
    owners, slots = index.shape
    return pl.pallas_call(
        rim_kernel,
        out_shape=(
            jax.ShapeDtypeStruct(h.shape, jnp.float32),
            jax.ShapeDtypeStruct((owners * slots, stack), jnp.float32),
        ),
        in_specs=[SMEM] + [ANY] * 5 + [VMEM] * 4,
        out_specs=(ANY, VMEM),
        input_output_aliases={5: 0},
        scratch_shapes=slab_scratch(2 * RIM, lateral, stack) + [
            pltpu.VMEM((track, lateral + 2 * EDGE, stack), jnp.float32),
            pltpu.SemaphoreType.DMA((4, 2)),
            pltpu.SemaphoreType.DMA,
            pltpu.SemaphoreType.DMA((2,)),
        ],
        compiler_params=pltpu.CompilerParams(vmem_limit_bytes=VMEM_ALL),
        cost_estimate=pl.CostEstimate(
            flops=50 * h.size, bytes_accessed=6 * h.size, transcendentals=4 * h.size
        ),
    )(index, h, k, bead, birth, part, *halos)


def shift(axis, by):
    count = lax.axis_size(axis)
    return [(i, i + by) for i in range(count) if 0 <= i + by < count]


def per_device(enthalpy, conductivity, bead_enthalpy, birth_time, send_rows, send_counts):
    lateral = enthalpy.shape[1]
    fields = (enthalpy, conductivity, bead_enthalpy, birth_time)

    to_low, to_high, to_left, to_right = strips(*fields)
    ylo = lax.ppermute(to_right, "gy", shift("gy", 1))
    yhi = lax.ppermute(to_left, "gy", shift("gy", -1))

    def with_corners(strip, cut):
        corners = [y[:, cut].reshape(3, HALO, HALO, -1).swapaxes(1, 2) for y in (ylo, yhi)]
        corners = jnp.concatenate(corners, 2).reshape(3 * HALO, 2 * HALO, -1)
        return lax.dynamic_update_slice(strip, corners, (0, lateral, 0))

    xlo = lax.ppermute(with_corners(to_high, slice(-HALO, None)), "gx", shift("gx", 1))
    xhi = lax.ppermute(with_corners(to_low, slice(0, HALO)), "gx", shift("gx", -1))

    rows, counts = send_rows[0, 0], send_counts[0, 0]
    slot = jnp.arange(rows.shape[1], dtype=jnp.int32)
    place = rows // lateral * (lateral + 2 * EDGE) + rows % lateral + EDGE
    index = jnp.where(slot[None, :] < counts[:, None], place, 0)

    part = inner_planes(*fields, ylo, yhi)
    end, outgoing = rim_and_rows(index, *fields, part, (xlo, xhi, ylo, yhi))
    outgoing = outgoing.reshape(rows.shape + outgoing.shape[1:])
    received = lax.all_to_all(outgoing, ("gx", "gy"), split_axis=0, concat_axis=0, tiled=True)
    return end, received.reshape(-1, received.shape[-1])


def solution(mesh):
    in_specs = (
        P("gx", "gy", None),
        P("gx", "gy", None),
        P("gx", "gy", None),
        P("gx", "gy", None),
        P("gx", "gy", None, None),
        P("gx", "gy", None),
    )
    out_specs = (P("gx", "gy", None), P(("gx", "gy"), None))
    return jax.shard_map(
        per_device, mesh=mesh, in_specs=in_specs, out_specs=out_specs, check_vma=False
    )
```

```python
import functools

import jax
import jax.numpy as jnp
from jax import lax
from jax.experimental import pallas as pl
from jax.experimental.pallas import tpu as pltpu
from jax.sharding import PartitionSpec as P

STEPS = 3
TICKS = 2000
LATENT = 0.5
SHARE = 0.2
TICK_SHARE = SHARE / TICKS

HALO = 3
EDGE = 8
LEAD = 4
LANES = 128
TILE = 8
OFFSET = 2.0
FAR = 1e-30
CHUNKS = 8
OUTS = 4
UNROLL = 4
ROLL_UP = 2
ROLL_DOWN = 2
PUN = 2
RIM = 3 * HALO
LIMIT = 60 * 1024 * 1024

HBM = pl.BlockSpec(memory_space=pl.ANY)
VMEM = pl.BlockSpec(memory_space=pltpu.VMEM)
SMEM = pl.BlockSpec(memory_space=pltpu.SMEM)


def kelvin(h):
    return jnp.minimum(h, jnp.maximum(h - LATENT, 1.0))


def lifted_kelvin(h):
    return jnp.minimum(h, jnp.maximum(h - LATENT, 1.0 + OFFSET))


def standing(h, bead, birth):
    return jnp.where((birth >= 0) & (birth < STEPS * TICKS), bead, h)


def face(one, two):
    return one[2] * two[2] * pl.reciprocal(one[1] + two[1], approx=True) * (two[0] - one[0])


def tile(j):
    return pl.ds(j * TILE, TILE)


class Slab:
    def __init__(self, raw, grids, rings, acc):
        self.raw = raw
        self.ha, self.hb, self.ks, self.kz, self.bs, self.bz = grids
        self.rings = rings
        self.acc = acc
        self.height = raw[0].shape[1]
        self.span = (self.height - 2 * (EDGE - LEAD)) // TILE

    def natural(self, j):
        return pl.ds(EDGE - LEAD + j, TILE, stride=self.span)

    def place(self, h, k, birth, x, rows):
        inside = k > 0.0
        values = (h, jnp.where(inside, k, 1.0), h, jnp.where(inside, birth, 1e6).astype(jnp.int32))
        for ref, value in zip(self.raw, values):
            ref[x, rows, :] = value

    def prepare(self, x):
        h_v, k_v, bead_v, birth_v = self.raw
        top = lax.broadcasted_iota(jnp.int32, (TILE, LANES), 1) == LANES - 1
        for j in range(self.span):
            at, to = self.natural(j), tile(j)
            birth, k = birth_v[x, at, :], k_v[x, at, :]
            b = birth.astype(jnp.float32) * TICK_SHARE
            self.ha[x, to, :] = standing(h_v[x, at, :], bead_v[x, at, :], birth) + OFFSET
            self.ks[x, to, :] = k
            self.kz[x, to, :] = jnp.where(top, FAR, pltpu.roll(k, LANES - 1, 1))
            self.bs[x, to, :] = b
            self.bz[x, to, :] = pltpu.roll(b, LANES - 1, 1)

    def prepare_all(self, lo, hi):
        @pl.loop(0, (hi - lo) // PUN)
        def _(i):
            for u in range(PUN):
                self.prepare(lo + i * PUN + u)

    def into(self, ref):
        def store(x, j, value):
            ref[x, tile(j), :] = value
        return store

    def run_step(self, step, src, store, base, cuts, before=None, after=None):
        span, acc, (ring_a, ring_b) = self.span, self.acc, self.rings

        def share(b):
            return jnp.clip(SHARE * (step + 1) - b, 0.0, SHARE)

        def point(x, j):
            at = tile(j)
            h = src[x, at, :]
            t = lifted_kelvin(h)
            return h, (t, pl.reciprocal(self.ks[x, at, :] * t, approx=True), share(self.bs[x, at, :]))

        def put(ring, j, values):
            for ref, value in zip(ring, values):
                ref[tile(j), :] = value

        def get(ring, j):
            return [ref[tile(j), :] for ref in ring]

        if before is not None:
            before(0)
        for j in range(span):
            last = point(base + cuts[0] - 1, j)[1]
            h, now = point(base + cuts[0], j)
            put(ring_a, j, now)
            acc[tile(j), :] = h - face(last, now)

        def planes(xs, rings):
            slots = []

            def load(x, here, there, j):
                cur = get(here, j)
                slot = dict(x=x, j=j, cur=cur, up=pltpu.roll(cur[0], LANES - 1, 1))
                if j == 0:
                    slot["beyond"] = [pltpu.roll(v, TILE - 1, 0) for v in cur]
                    slot["fy_old"] = pltpu.roll(face(get(here, span - 1), slot["beyond"]), 1, 0)
                slot["h"], slot["nxt"] = point(x + 1, j)
                put(there, j, slot["nxt"])
                return slot

            def work(n):
                slot = slots[n]
                x, j, cur, t = slot["x"], slot["j"], slot["cur"], slot["up"]
                at = tile(j)
                fx = face(cur, slot["nxt"])
                total = acc[at, :] + fx
                acc[at, :] = slot["h"] - fx
                last = j + 1 == span
                fy = face(cur, slots[n - j]["beyond"] if last else slots[n + 1]["cur"])
                if not last:
                    slots[n + 1]["fy_old"] = fy
                fz = face(
                    cur, (t, pl.reciprocal(self.kz[x, at, :] * t, approx=True), share(self.bz[x, at, :]))
                )
                slot["total"] = total + ((fy - slot["fy_old"]) + fz)
                slot["down"] = pltpu.roll(fz, 1, 1)

            def done(n):
                slot = slots[n]
                store(slot["x"], slot["j"], slot["total"] - slot["down"])

            todo = [(x, *pair, j) for x, pair in zip(xs, rings) for j in range(span)]
            for n in range(len(todo) + ROLL_UP + ROLL_DOWN):
                if n < len(todo):
                    slots.append(load(*todo[n]))
                if 0 <= n - ROLL_UP < len(todo):
                    work(n - ROLL_UP)
                if 0 <= n - ROLL_UP - ROLL_DOWN:
                    done(n - ROLL_UP - ROLL_DOWN)

        both = [(ring_a, ring_b), (ring_b, ring_a)]
        for n, (lo, hi) in enumerate(zip(cuts[:-1], cuts[1:])):
            unroll = UNROLL if (hi - lo) % UNROLL == 0 else 2
            if n and before is not None:
                before(n)

            @pl.loop(0, (hi - lo) // unroll)
            def _(i):
                planes([base + lo + unroll * i + u for u in range(unroll)], both * (unroll // 2))

            if (hi - lo) % 2:
                planes([base + hi - 1], both[:1])
            if after is not None:
                after(n)


def slab_scratch(planes, lateral, stack):
    tiles = (lateral + 2 * LEAD, stack)
    raw = (planes, lateral + 2 * EDGE, stack)
    return [
        [pltpu.VMEM(raw, dtype) for dtype in (jnp.float32, jnp.float32, jnp.float32, jnp.int32)],
        [pltpu.VMEM((planes,) + tiles, jnp.float32)] * 6,
        [[pltpu.VMEM(tiles, jnp.float32)] * 3] * 2,
        pltpu.VMEM(tiles, jnp.float32),
    ]


def lateral_kernel(h_hbm, k_hbm, bead_hbm, birth_hbm, lo_ref, hi_ref, ys, sem):
    track, lateral, _ = h_hbm.shape
    copies = [
        pltpu.make_async_copy(hbm.at[:, pl.ds(side * (lateral - EDGE), EDGE)], ys[i].at[side], sem.at[i, side])
        for i, hbm in enumerate((h_hbm, k_hbm, bead_hbm, birth_hbm)) for side in range(2)
    ]
    for copy in copies:
        copy.start()
    for copy in copies:
        copy.wait()
    flat = [ref.reshape(2 * track * EDGE, LANES) for ref in ys]
    for side, out in ((0, lo_ref), (1, hi_ref)):
        for i in range(track // TILE):
            for d in range(HALO):
                row = (side * track + i * TILE) * EDGE + d + side * (EDGE - HALO)
                h, k, bead, birth = [ref[pl.ds(row, TILE, stride=EDGE), :] for ref in flat]
                out[d, tile(i), :] = standing(h, bead, birth)
                out[HALO + d, tile(i), :] = k
                out[2 * HALO + d, tile(i), :] = birth.astype(jnp.float32)


def track_kernel(h_hbm, k_hbm, bead_hbm, birth_hbm, lo_ref, hi_ref, xs, sem):
    track, lateral, _ = h_hbm.shape
    copies = [
        pltpu.make_async_copy(hbm.at[pl.ds(side * (track - HALO), HALO)], xs[i].at[side], sem.at[i, side])
        for i, hbm in enumerate((h_hbm, k_hbm, bead_hbm, birth_hbm)) for side in range(2)
    ]
    for copy in copies:
        copy.start()
    for copy in copies:
        copy.wait()
    rows = pl.ds(0, lateral)
    for side, out in ((0, lo_ref), (1, hi_ref)):
        @pl.loop(0, HALO)
        def _(d, side=side, out=out):
            birth = xs[3][side, d]
            out[d, rows, :] = standing(xs[0][side, d], xs[2][side, d], birth)
            out[HALO + d, rows, :] = xs[1][side, d]
            out[2 * HALO + d, rows, :] = birth.astype(jnp.float32)


def strips(kernel, fields, length, held):
    stack = fields[0].shape[2]
    out = jax.ShapeDtypeStruct((3 * HALO, length, stack), jnp.float32)
    return pl.pallas_call(
        kernel,
        out_shape=(out, out),
        in_specs=[HBM] * 4,
        out_specs=(VMEM,) * 2,
        scratch_shapes=[
            [pltpu.VMEM((2,) + held, field.dtype) for field in fields],
            pltpu.SemaphoreType.DMA((4, 2)),
        ],
        compiler_params=pltpu.CompilerParams(vmem_limit_bytes=LIMIT),
    )(*fields)


def corner_kernel(low_in, high_in, ylo_ref, yhi_ref, low_out, high_out, held, sem):
    del low_in, high_in
    track = ylo_ref.shape[1]
    copies = []
    for side, out in ((0, low_out), (1, high_out)):
        for f in range(3):
            for d in range(HALO):
                at = pl.ds(side * (track - HALO) + d, 1)
                for y, ref in enumerate((ylo_ref, yhi_ref)):
                    for e in range(HALO):
                        held[side, f * HALO + d, pl.ds(y * HALO + e, 1), :] = ref[f * HALO + e, at, :]
        rows = pl.ds(out.shape[1] - EDGE, EDGE)
        copies.append(pltpu.make_async_copy(held.at[side], out.at[:, rows], sem.at[side]))
        copies[-1].start()
    for copy in copies:
        copy.wait()


def corners(low, high, ylo, yhi):
    return pl.pallas_call(
        corner_kernel,
        out_shape=(jax.ShapeDtypeStruct(low.shape, low.dtype),) * 2,
        in_specs=[HBM] * 2 + [VMEM] * 2,
        out_specs=(HBM,) * 2,
        input_output_aliases={0: 0, 1: 1},
        scratch_shapes=[
            pltpu.VMEM((2, 3 * HALO, EDGE, LANES), jnp.float32),
            pltpu.SemaphoreType.DMA((2,)),
        ],
        compiler_params=pltpu.CompilerParams(vmem_limit_bytes=LIMIT),
    )(low, high, ylo, yhi)


def inner_kernel(
    h_hbm, k_hbm, bead_hbm, birth_hbm, ylo_ref, yhi_ref, out_hbm, raw, grids, rings, acc, sem_in, sem_out
):
    track, lateral, _ = h_hbm.shape
    slab = Slab(raw, grids, rings, acc)
    inner = pl.ds(EDGE, lateral)
    piece = track // CHUNKS

    def copies(n):
        at = pl.ds(n * piece, piece)
        return [
            pltpu.make_async_copy(hbm.at[at], vmem.at[at, inner], sem_in.at[i, n])
            for i, (hbm, vmem) in enumerate(zip((h_hbm, k_hbm, bead_hbm, birth_hbm), raw))
        ]

    for n in range(CHUNKS):
        for copy in copies(n):
            copy.start()

    height = lateral + 2 * EDGE
    flat = [ref.reshape(track * height, LANES) for ref in raw]
    for ref, first in ((ylo_ref, EDGE - HALO), (yhi_ref, EDGE + lateral)):
        @pl.loop(0, track // TILE)
        def _(i, ref=ref, first=first):
            for d in range(HALO):
                h, k, birth = [ref[f * HALO + d, pl.ds(i * TILE, TILE), :] for f in range(3)]
                at = pl.ds(i * TILE * height + first + d, TILE, stride=height)
                inside = k > 0.0
                flat[0][at, :] = h
                flat[1][at, :] = jnp.where(inside, k, 1.0)
                flat[2][at, :] = h
                flat[3][at, :] = jnp.where(inside, birth, 1e6).astype(jnp.int32)

    def arrive(n):
        for copy in copies(n):
            copy.wait()
        slab.prepare_all(n * piece, (n + 1) * piece)

    cuts = [HALO] + [n * (track // OUTS) + HALO for n in range(1, OUTS)] + [track - HALO]

    def out_copy(n):
        at = pl.ds(cuts[n], cuts[n + 1] - cuts[n])
        return pltpu.make_async_copy(raw[0].at[at, inner], out_hbm.at[at], sem_out.at[n])

    def finish(x, j, value):
        raw[0][x, slab.natural(j), :] = value - OFFSET

    arrivals = [1] + [n * piece - 1 for n in range(1, CHUNKS + 1)]
    slab.run_step(0, slab.ha, slab.into(slab.hb), 0, arrivals, before=arrive)
    slab.run_step(1, slab.hb, slab.into(slab.ha), 0, (2, track - 2))
    slab.run_step(2, slab.ha, finish, 0, cuts, after=lambda n: out_copy(n).start())
    for n in range(OUTS):
        out_copy(n).wait()


def inner_planes(h, k, bead, birth, ylo, yhi):
    track, lateral, stack = h.shape
    return pl.pallas_call(
        inner_kernel,
        out_shape=jax.ShapeDtypeStruct(h.shape, jnp.float32),
        in_specs=[HBM] * 4 + [VMEM] * 2,
        out_specs=HBM,
        scratch_shapes=slab_scratch(track, lateral, stack) + [
            pltpu.SemaphoreType.DMA((4, CHUNKS)),
            pltpu.SemaphoreType.DMA((OUTS,)),
        ],
        compiler_params=pltpu.CompilerParams(vmem_limit_bytes=LIMIT),
        cost_estimate=pl.CostEstimate(
            flops=200 * h.size, bytes_accessed=20 * h.size, transcendentals=15 * h.size
        ),
    )(h, k, bead, birth, ylo, yhi)


def rim_kernel(
    index_ref, h_hbm, k_hbm, bead_hbm, birth_hbm, part_hbm, xlo_ref, xhi_ref, ylo_ref, yhi_ref,
    out_hbm, rows_ref, raw, grids, rings, acc, whole, sem_in, sem_part, sem_out,
):
    track, lateral, _ = h_hbm.shape
    slab = Slab(raw, grids, rings, acc)
    inner = pl.ds(EDGE, lateral)
    own = RIM - HALO

    copies = []
    for i, (hbm, vmem) in enumerate(zip((h_hbm, k_hbm, bead_hbm, birth_hbm), raw)):
        for side in range(2):
            src = pl.ds(side * (track - own), own)
            dst = pl.ds(HALO + side * own, own)
            copies.append(pltpu.make_async_copy(hbm.at[src], vmem.at[dst, inner], sem_in.at[i, side]))
    for copy in copies:
        copy.start()
    middle = pl.ds(HALO, track - 2 * HALO)
    part = pltpu.make_async_copy(part_hbm.at[middle], whole.at[middle, inner], sem_part)
    part.start()

    below, above = pl.ds(EDGE - HALO, HALO), pl.ds(EDGE + lateral, HALO)
    for side, ref in ((0, xlo_ref), (1, xhi_ref)):
        @pl.loop(0, HALO)
        def _(d, side=side, ref=ref):
            for first, n, rows in ((0, lateral, inner), (lateral, HALO, below), (lateral + HALO, HALO, above)):
                slab.place(
                    *[ref[f * HALO + d, pl.ds(first, n), :] for f in range(3)], side * (RIM + own) + d, rows
                )
    for x in range(HALO, HALO + 2 * own):
        at = pl.ds(x - HALO + (track - 2 * own if x >= RIM else 0), 1)
        for y, ref in enumerate((ylo_ref, yhi_ref)):
            for d in range(HALO):
                row = pl.ds((EDGE - HALO, EDGE + lateral)[y] + d, 1)
                slab.place(*[ref[f * HALO + d, at, :] for f in range(3)], x, row)

    for copy in copies:
        copy.wait()
    slab.prepare_all(0, 2 * RIM)

    def finish(x, j, value):
        at = x - HALO + jnp.where(x >= RIM, track - 2 * own, 0)
        whole[at, slab.natural(j), :] = value - OFFSET

    @pl.loop(0, 2)
    def _(side):
        base = side * RIM
        slab.run_step(0, slab.ha, slab.into(slab.hb), base, (1, RIM - 1))
        slab.run_step(1, slab.hb, slab.into(slab.ha), base, (2, RIM - 2))
        slab.run_step(2, slab.ha, finish, base, (3, RIM - 3))

    outs = []
    for side in range(2):
        at = pl.ds(side * (track - HALO), HALO)
        outs.append(pltpu.make_async_copy(whole.at[at, inner], out_hbm.at[at], sem_out.at[side]))
    for copy in outs:
        copy.start()
    part.wait()

    whole[0, 0:EDGE, :] = jnp.zeros((EDGE, LANES), jnp.float32)
    owners, slots = index_ref.shape
    flat = whole.reshape(track * (lateral + 2 * EDGE), LANES)

    @pl.loop(0, owners)
    def _(o):
        for k in range(slots):
            rows_ref[pl.ds(o * slots + k, 1), :] = kelvin(flat[pl.ds(index_ref[o, k], 1), :])

    for copy in outs:
        copy.wait()


def rim_and_rows(index, h, k, bead, birth, part, halos):
    track, lateral, stack = h.shape
    owners, slots = index.shape
    return pl.pallas_call(
        rim_kernel,
        out_shape=(
            jax.ShapeDtypeStruct(h.shape, jnp.float32),
            jax.ShapeDtypeStruct((owners * slots, stack), jnp.float32),
        ),
        in_specs=[SMEM] + [HBM] * 5 + [VMEM] * 4,
        out_specs=(HBM, VMEM),
        input_output_aliases={5: 0},
        scratch_shapes=slab_scratch(2 * RIM, lateral, stack) + [
            pltpu.VMEM((track, lateral + 2 * EDGE, stack), jnp.float32),
            pltpu.SemaphoreType.DMA((4, 2)),
            pltpu.SemaphoreType.DMA,
            pltpu.SemaphoreType.DMA((2,)),
        ],
        compiler_params=pltpu.CompilerParams(vmem_limit_bytes=LIMIT),
        cost_estimate=pl.CostEstimate(
            flops=50 * h.size, bytes_accessed=6 * h.size, transcendentals=4 * h.size
        ),
    )(index, h, k, bead, birth, part, *halos)


def shift(axis, by):
    count = lax.axis_size(axis)
    return [(i, i + by) for i in range(count) if 0 <= i + by < count]


def per_device(enthalpy, conductivity, bead_enthalpy, birth_time, send_rows, send_counts):
    fields = (enthalpy, conductivity, bead_enthalpy, birth_time)

    track, lateral, stack = enthalpy.shape
    to_left, to_right = strips(lateral_kernel, fields, track, (track, EDGE, stack))
    to_low, to_high = strips(track_kernel, fields, lateral + EDGE, (HALO, lateral, stack))
    ylo = lax.ppermute(to_right, "gy", shift("gy", 1))
    yhi = lax.ppermute(to_left, "gy", shift("gy", -1))

    to_low, to_high = corners(to_low, to_high, ylo, yhi)
    xlo = lax.ppermute(to_high, "gx", shift("gx", 1))
    xhi = lax.ppermute(to_low, "gx", shift("gx", -1))

    rows, counts = send_rows[0, 0], send_counts[0, 0]
    slot = jnp.arange(rows.shape[1], dtype=jnp.int32)
    place = rows // lateral * (lateral + 2 * EDGE) + rows % lateral + EDGE
    index = jnp.where(slot[None, :] < counts[:, None], place, 0)

    part = inner_planes(*fields, ylo, yhi)
    end, outgoing = rim_and_rows(index, *fields, part, (xlo, xhi, ylo, yhi))
    outgoing = outgoing.reshape(rows.shape + outgoing.shape[1:])
    received = lax.all_to_all(outgoing, ("gx", "gy"), split_axis=0, concat_axis=0, tiled=True)
    return end, received.reshape(-1, received.shape[-1])


def solution(mesh):
    in_specs = (
        P("gx", "gy", None),
        P("gx", "gy", None),
        P("gx", "gy", None),
        P("gx", "gy", None),
        P("gx", "gy", None, None),
        P("gx", "gy", None),
    )
    out_specs = (P("gx", "gy", None), P(("gx", "gy"), None))
    return jax.shard_map(
        per_device, mesh=mesh, in_specs=in_specs, out_specs=out_specs, check_vma=False
    )
```

```python
import functools

import jax
import jax.numpy as jnp
from jax import lax
from jax.experimental import pallas as pl
from jax.experimental.pallas import tpu as pltpu
from jax.sharding import PartitionSpec as P

STEPS = 3
TICKS = 2000
LATENT = 0.5
SHARE = 0.2
TICK_SHARE = SHARE / TICKS

HALO = 3
EDGE = 8
LEAD = 4
LANES = 128
TILE = 8
OFFSET = 2.0
FAR = 1e-30
CHUNKS = 8
OUTS = 4
UNROLL = 4
ROLL_UP = 2
ROLL_DOWN = 2
PUN = 2
RIM = 3 * HALO
HANDED = ((0, 2), (1, 2), (2, 2), (0, 4), (0, 4), (0, 4), (0, 4))
MIB = 1024 * 1024
RIM_LIMIT = 24 * MIB
LIMIT = 60 * MIB

HBM = pl.BlockSpec(memory_space=pl.ANY)
VMEM = pl.BlockSpec(memory_space=pltpu.VMEM)
SMEM = pl.BlockSpec(memory_space=pltpu.SMEM)


def kelvin(h):
    return jnp.minimum(h, jnp.maximum(h - LATENT, 1.0))


def lifted_kelvin(h):
    return jnp.minimum(h, jnp.maximum(h - LATENT, 1.0 + OFFSET))


def standing(h, bead, birth):
    return jnp.where((birth >= 0) & (birth < STEPS * TICKS), bead, h)


def face(one, two):
    return one[2] * two[2] * pl.reciprocal(one[1] + two[1], approx=True) * (two[0] - one[0])


def tile(j):
    return pl.ds(j * TILE, TILE)


class Slab:
    def __init__(self, raw, grids, rings, acc):
        self.raw = raw
        self.ha, self.hb, self.ks, self.kz, self.bs, self.bz = grids
        self.rings = rings
        self.acc = acc
        self.height = raw[0].shape[1]
        self.span = (self.height - 2 * (EDGE - LEAD)) // TILE

    def natural(self, j):
        return pl.ds(EDGE - LEAD + j, TILE, stride=self.span)

    def place(self, h, k, birth, x, rows):
        inside = k > 0.0
        values = (h, jnp.where(inside, k, 1.0), h, jnp.where(inside, birth, 1e6).astype(jnp.int32))
        for ref, value in zip(self.raw, values):
            ref[x, rows, :] = value

    def prepare(self, x, to_x):
        h_v, k_v, bead_v, birth_v = self.raw
        top = lax.broadcasted_iota(jnp.int32, (TILE, LANES), 1) == LANES - 1
        for j in range(self.span):
            at, to = self.natural(j), tile(j)
            birth, k = birth_v[x, at, :], k_v[x, at, :]
            b = birth.astype(jnp.float32) * TICK_SHARE
            self.ha[to_x, to, :] = standing(h_v[x, at, :], bead_v[x, at, :], birth) + OFFSET
            self.ks[to_x, to, :] = k
            self.kz[to_x, to, :] = jnp.where(top, FAR, pltpu.roll(k, LANES - 1, 1))
            self.bs[to_x, to, :] = b
            self.bz[to_x, to, :] = pltpu.roll(b, LANES - 1, 1)

    def prepare_all(self, lo, hi):
        @pl.loop(0, (hi - lo) // PUN)
        def _(i):
            for u in range(PUN):
                self.prepare(lo + i * PUN + u, lo + i * PUN + u)

    def into(self, ref):
        def store(x, j, value):
            ref[x, tile(j), :] = value
        return store

    def run_step(self, step, src, store, base, cuts, before=None, after=None):
        span, acc, (ring_a, ring_b) = self.span, self.acc, self.rings

        def share(b):
            return jnp.clip(SHARE * (step + 1) - b, 0.0, SHARE)

        def point(x, j):
            at = tile(j)
            h = src[x, at, :]
            t = lifted_kelvin(h)
            return h, (t, pl.reciprocal(self.ks[x, at, :] * t, approx=True), share(self.bs[x, at, :]))

        def put(ring, j, values):
            for ref, value in zip(ring, values):
                ref[tile(j), :] = value

        def get(ring, j):
            return [ref[tile(j), :] for ref in ring]

        if before is not None:
            before(0)
        for j in range(span):
            last = point(base + cuts[0] - 1, j)[1]
            h, now = point(base + cuts[0], j)
            put(ring_a, j, now)
            acc[tile(j), :] = h - face(last, now)

        def planes(xs, rings):
            slots = []

            def load(x, here, there, j):
                cur = get(here, j)
                slot = dict(x=x, j=j, cur=cur, up=pltpu.roll(cur[0], LANES - 1, 1))
                if j == 0:
                    slot["beyond"] = [pltpu.roll(v, TILE - 1, 0) for v in cur]
                    slot["fy_old"] = pltpu.roll(face(get(here, span - 1), slot["beyond"]), 1, 0)
                slot["h"], slot["nxt"] = point(x + 1, j)
                put(there, j, slot["nxt"])
                return slot

            def work(n):
                slot = slots[n]
                x, j, cur, t = slot["x"], slot["j"], slot["cur"], slot["up"]
                at = tile(j)
                fx = face(cur, slot["nxt"])
                total = acc[at, :] + fx
                acc[at, :] = slot["h"] - fx
                last = j + 1 == span
                fy = face(cur, slots[n - j]["beyond"] if last else slots[n + 1]["cur"])
                if not last:
                    slots[n + 1]["fy_old"] = fy
                fz = face(
                    cur, (t, pl.reciprocal(self.kz[x, at, :] * t, approx=True), share(self.bz[x, at, :]))
                )
                slot["total"] = total + ((fy - slot["fy_old"]) + fz)
                slot["down"] = pltpu.roll(fz, 1, 1)

            def done(n):
                slot = slots[n]
                store(slot["x"], slot["j"], slot["total"] - slot["down"])

            todo = [(x, *pair, j) for x, pair in zip(xs, rings) for j in range(span)]
            for n in range(len(todo) + ROLL_UP + ROLL_DOWN):
                if n < len(todo):
                    slots.append(load(*todo[n]))
                if 0 <= n - ROLL_UP < len(todo):
                    work(n - ROLL_UP)
                if 0 <= n - ROLL_UP - ROLL_DOWN:
                    done(n - ROLL_UP - ROLL_DOWN)

        both = [(ring_a, ring_b), (ring_b, ring_a)]
        for n, (lo, hi) in enumerate(zip(cuts[:-1], cuts[1:])):
            if hi - lo == HALO:
                planes([base + x for x in range(lo, hi)], (both * HALO)[:HALO])
                continue
            unroll = UNROLL if (hi - lo) % UNROLL == 0 else 2
            if n and before is not None:
                before(n)

            @pl.loop(0, (hi - lo) // unroll)
            def _(i):
                planes([base + lo + unroll * i + u for u in range(unroll)], both * (unroll // 2))

            if after is not None:
                after(n)


def slab_scratch(raw_planes, planes, lateral, stack):
    tiles = (lateral + 2 * LEAD, stack)
    raw = (raw_planes, lateral + 2 * EDGE, stack)
    return [
        [pltpu.VMEM(raw, dtype) for dtype in (jnp.float32, jnp.float32, jnp.float32, jnp.int32)],
        [pltpu.VMEM((planes,) + tiles, jnp.float32)] * 6,
        [[pltpu.VMEM(tiles, jnp.float32)] * 3] * 2,
        pltpu.VMEM(tiles, jnp.float32),
    ]


def lateral_kernel(h_hbm, k_hbm, bead_hbm, birth_hbm, lo_ref, hi_ref, ys, sem):
    track, lateral, _ = h_hbm.shape
    copies = [
        pltpu.make_async_copy(hbm.at[:, pl.ds(side * (lateral - EDGE), EDGE)], ys[i].at[side], sem.at[i, side])
        for i, hbm in enumerate((h_hbm, k_hbm, bead_hbm, birth_hbm)) for side in range(2)
    ]
    for copy in copies:
        copy.start()
    for copy in copies:
        copy.wait()
    flat = [ref.reshape(2 * track * EDGE, LANES) for ref in ys]
    for side, out in ((0, lo_ref), (1, hi_ref)):
        for i in range(track // TILE):
            for d in range(HALO):
                row = (side * track + i * TILE) * EDGE + d + side * (EDGE - HALO)
                h, k, bead, birth = [ref[pl.ds(row, TILE, stride=EDGE), :] for ref in flat]
                out[d, tile(i), :] = standing(h, bead, birth)
                out[HALO + d, tile(i), :] = k
                out[2 * HALO + d, tile(i), :] = birth.astype(jnp.float32)


def track_kernel(h_hbm, k_hbm, bead_hbm, birth_hbm, lo_ref, hi_ref, xs, sem):
    track, lateral, _ = h_hbm.shape
    copies = [
        pltpu.make_async_copy(hbm.at[pl.ds(side * (track - HALO), HALO)], xs[i].at[side], sem.at[i, side])
        for i, hbm in enumerate((h_hbm, k_hbm, bead_hbm, birth_hbm)) for side in range(2)
    ]
    for copy in copies:
        copy.start()
    for copy in copies:
        copy.wait()
    rows = pl.ds(0, lateral)
    for side, out in ((0, lo_ref), (1, hi_ref)):
        @pl.loop(0, HALO)
        def _(d, side=side, out=out):
            birth = xs[3][side, d]
            out[d, rows, :] = standing(xs[0][side, d], xs[2][side, d], birth)
            out[HALO + d, rows, :] = xs[1][side, d]
            out[2 * HALO + d, rows, :] = birth.astype(jnp.float32)


def strips(kernel, fields, length, held):
    stack = fields[0].shape[2]
    out = jax.ShapeDtypeStruct((3 * HALO, length, stack), jnp.float32)
    return pl.pallas_call(
        kernel,
        out_shape=(out, out),
        in_specs=[HBM] * 4,
        out_specs=(VMEM,) * 2,
        scratch_shapes=[
            [pltpu.VMEM((2,) + held, field.dtype) for field in fields],
            pltpu.SemaphoreType.DMA((4, 2)),
        ],
        compiler_params=pltpu.CompilerParams(vmem_limit_bytes=LIMIT),
    )(*fields)


def corner_kernel(low_in, high_in, ylo_ref, yhi_ref, low_out, high_out, held, sem):
    del low_in, high_in
    track = ylo_ref.shape[1]
    copies = []
    for side, out in ((0, low_out), (1, high_out)):
        for f in range(3):
            for d in range(HALO):
                at = pl.ds(side * (track - HALO) + d, 1)
                for y, ref in enumerate((ylo_ref, yhi_ref)):
                    for e in range(HALO):
                        held[side, f * HALO + d, pl.ds(y * HALO + e, 1), :] = ref[f * HALO + e, at, :]
        rows = pl.ds(out.shape[1] - EDGE, EDGE)
        copies.append(pltpu.make_async_copy(held.at[side], out.at[:, rows], sem.at[side]))
        copies[-1].start()
    for copy in copies:
        copy.wait()


def corners(low, high, ylo, yhi):
    return pl.pallas_call(
        corner_kernel,
        out_shape=(jax.ShapeDtypeStruct(low.shape, low.dtype),) * 2,
        in_specs=[HBM] * 2 + [VMEM] * 2,
        out_specs=(HBM,) * 2,
        input_output_aliases={0: 0, 1: 1},
        scratch_shapes=[
            pltpu.VMEM((2, 3 * HALO, EDGE, LANES), jnp.float32),
            pltpu.SemaphoreType.DMA((2,)),
        ],
        compiler_params=pltpu.CompilerParams(vmem_limit_bytes=8 * MIB),
    )(low, high, ylo, yhi)


def inner_kernel(
    h_hbm, k_hbm, bead_hbm, birth_hbm, ylo_ref, yhi_ref, out_hbm, *rest
):
    handed, (raw, grids, rings, acc, sem_in, sem_out, sem_hand) = rest[:7], rest[7:]
    track, lateral, _ = h_hbm.shape
    slab = Slab(raw, grids, rings, acc)
    inner = pl.ds(EDGE, lateral)
    piece = track // CHUNKS

    def copies(n):
        at = pl.ds(n * piece, piece)
        return [
            pltpu.make_async_copy(hbm.at[at], vmem.at[at, inner], sem_in.at[i, n])
            for i, (hbm, vmem) in enumerate(zip((h_hbm, k_hbm, bead_hbm, birth_hbm), raw))
        ]

    for n in range(CHUNKS):
        for copy in copies(n):
            copy.start()

    height = lateral + 2 * EDGE
    flat = [ref.reshape(track * height, LANES) for ref in raw]
    for ref, first in ((ylo_ref, EDGE - HALO), (yhi_ref, EDGE + lateral)):
        @pl.loop(0, track // TILE)
        def _(i, ref=ref, first=first):
            for d in range(HALO):
                h, k, birth = [ref[f * HALO + d, pl.ds(i * TILE, TILE), :] for f in range(3)]
                at = pl.ds(i * TILE * height + first + d, TILE, stride=height)
                inside = k > 0.0
                flat[0][at, :] = h
                flat[1][at, :] = jnp.where(inside, k, 1.0)
                flat[2][at, :] = h
                flat[3][at, :] = jnp.where(inside, birth, 1e6).astype(jnp.int32)

    def arrive(n):
        for copy in copies(n):
            copy.wait()
        slab.prepare_all(n * piece, (n + 1) * piece)

    cuts = [HALO] + [n * (track // OUTS) + HALO for n in range(1, OUTS)] + [track - HALO]

    def out_copy(n):
        at = pl.ds(cuts[n], cuts[n + 1] - cuts[n])
        return pltpu.make_async_copy(raw[0].at[at, inner], out_hbm.at[at], sem_out.at[n])

    def finish(x, j, value):
        raw[0][x, slab.natural(j), :] = value - OFFSET

    arrivals = [1] + [n * piece - 1 for n in range(1, CHUNKS + 1)]
    def hand(i):
        ref, (first, count) = (slab.ha, slab.hb, slab.ha, *grids[2:])[i], HANDED[i]
        return [
            pltpu.make_async_copy(
                ref.at[pl.ds((first, track - first - count)[side], count)], handed[i].at[side], sem_hand.at[i, side]
            )
            for side in range(2)
        ]

    slab.run_step(0, slab.ha, slab.into(slab.hb), 0, arrivals, before=arrive)
    for i in (0, 1, 3, 4, 5, 6):
        for copy in hand(i):
            copy.start()
    slab.run_step(1, slab.hb, slab.into(slab.ha), 0, (2, track - 2))
    for copy in hand(2):
        copy.start()
    slab.run_step(2, slab.ha, finish, 0, cuts, after=lambda n: out_copy(n).start())
    for n in range(OUTS):
        out_copy(n).wait()
    for i in range(len(HANDED)):
        for copy in hand(i):
            copy.wait()


def inner_planes(h, k, bead, birth, ylo, yhi):
    track, lateral, stack = h.shape
    return pl.pallas_call(
        inner_kernel,
        out_shape=(
            jax.ShapeDtypeStruct(h.shape, jnp.float32),
            *[jax.ShapeDtypeStruct((2, n, lateral + 2 * LEAD, stack), jnp.float32) for _, n in HANDED],
        ),
        in_specs=[HBM] * 4 + [VMEM] * 2,
        out_specs=(HBM,) * (1 + len(HANDED)),
        scratch_shapes=slab_scratch(track, track, lateral, stack) + [
            pltpu.SemaphoreType.DMA((4, CHUNKS)),
            pltpu.SemaphoreType.DMA((OUTS,)),
            pltpu.SemaphoreType.DMA((len(HANDED), 2)),
        ],
        compiler_params=pltpu.CompilerParams(vmem_limit_bytes=50 * MIB),
        cost_estimate=pl.CostEstimate(
            flops=200 * h.size, bytes_accessed=20 * h.size, transcendentals=15 * h.size
        ),
    )(h, k, bead, birth, ylo, yhi)


def rim_kernel(index_ref, part_hbm, xlo_ref, xhi_ref, *rest):
    handed, (out_hbm, rows_ref, raw, grids, rings, acc, whole, sem_in, sem_part, sem_out) = rest[:7], rest[7:]
    track, lateral, _ = part_hbm.shape
    slab = Slab(raw, grids, rings, acc)
    inner = pl.ds(EDGE, lateral)
    own = RIM - HALO

    copies = []
    for i, (first, count) in enumerate(HANDED):
        ref = (slab.ha, slab.hb, slab.ha, *grids[2:])[i]
        for side in range(2):
            dst = (HALO + first, RIM + own - first - count)[side]
            copies.append(
                pltpu.make_async_copy(handed[i].at[side], ref.at[pl.ds(dst, count)], sem_in.at[i, side])
            )
    for copy in copies:
        copy.start()
    middle = pl.ds(HALO, track - 2 * HALO)
    part = pltpu.make_async_copy(part_hbm.at[middle], whole.at[middle, inner], sem_part)
    part.start()

    below, above = pl.ds(EDGE - HALO, HALO), pl.ds(EDGE + lateral, HALO)
    for side, ref in ((0, xlo_ref), (1, xhi_ref)):
        for d in range(HALO):
            for first, n, rows in ((0, lateral, inner), (lateral, HALO, below), (lateral + HALO, HALO, above)):
                slab.place(*[ref[f * HALO + d, pl.ds(first, n), :] for f in range(3)], side * HALO + d, rows)
    for side in range(2):
        for d in range(HALO):
            slab.prepare(side * HALO + d, side * (RIM + own) + d)
    for copy in copies:
        copy.wait()

    def finish(x, j, value):
        at = x - HALO + jnp.where(x >= RIM, track - 2 * own, 0)
        whole[at, slab.natural(j), :] = value - OFFSET

    @pl.loop(0, 2)
    def _(side):
        stores = (slab.into(slab.hb), slab.into(slab.ha), finish)
        for step, (src, store) in enumerate(zip((slab.ha, slab.hb, slab.ha), stores)):
            first = 1 + step
            last = 2 * RIM - first - HALO
            slab.run_step(step, src, store, side * (last - first), (first, first + HALO))

    outs = []
    for side in range(2):
        at = pl.ds(side * (track - HALO), HALO)
        outs.append(pltpu.make_async_copy(whole.at[at, inner], out_hbm.at[at], sem_out.at[side]))
    for copy in outs:
        copy.start()
    part.wait()

    whole[0, 0:EDGE, :] = jnp.zeros((EDGE, LANES), jnp.float32)
    owners, slots = index_ref.shape
    flat = whole.reshape(track * (lateral + 2 * EDGE), LANES)

    @pl.loop(0, owners)
    def _(o):
        for k in range(slots):
            rows_ref[pl.ds(o * slots + k, 1), :] = kelvin(flat[pl.ds(index_ref[o, k], 1), :])

    for copy in outs:
        copy.wait()


def rim_and_rows(index, part, xlo, xhi, handed):
    track, lateral, stack = part.shape
    owners, slots = index.shape
    return pl.pallas_call(
        rim_kernel,
        out_shape=(
            jax.ShapeDtypeStruct(part.shape, jnp.float32),
            jax.ShapeDtypeStruct((owners * slots, stack), jnp.float32),
        ),
        in_specs=[SMEM, HBM] + [VMEM] * 2 + [HBM] * len(HANDED),
        out_specs=(HBM, VMEM),
        input_output_aliases={1: 0},
        scratch_shapes=slab_scratch(2 * HALO, 2 * RIM, lateral, stack) + [
            pltpu.VMEM((track, lateral + 2 * EDGE, stack), jnp.float32),
            pltpu.SemaphoreType.DMA((len(HANDED), 2)),
            pltpu.SemaphoreType.DMA,
            pltpu.SemaphoreType.DMA((2,)),
        ],
        compiler_params=pltpu.CompilerParams(vmem_limit_bytes=RIM_LIMIT),
        cost_estimate=pl.CostEstimate(
            flops=30 * part.size, bytes_accessed=3 * part.size, transcendentals=3 * part.size
        ),
    )(index, part, xlo, xhi, *handed)


def shift(axis, by):
    count = lax.axis_size(axis)
    return [(i, i + by) for i in range(count) if 0 <= i + by < count]


def per_device(enthalpy, conductivity, bead_enthalpy, birth_time, send_rows, send_counts):
    fields = (enthalpy, conductivity, bead_enthalpy, birth_time)

    track, lateral, stack = enthalpy.shape
    to_left, to_right = strips(lateral_kernel, fields, track, (track, EDGE, stack))
    to_low, to_high = strips(track_kernel, fields, lateral + EDGE, (HALO, lateral, stack))
    ylo = lax.ppermute(to_right, "gy", shift("gy", 1))
    yhi = lax.ppermute(to_left, "gy", shift("gy", -1))

    to_low, to_high = corners(to_low, to_high, ylo, yhi)
    xlo = lax.ppermute(to_high, "gx", shift("gx", 1))
    xhi = lax.ppermute(to_low, "gx", shift("gx", -1))

    rows, counts = send_rows[0, 0], send_counts[0, 0]
    slot = jnp.arange(rows.shape[1], dtype=jnp.int32)
    place = rows // lateral * (lateral + 2 * EDGE) + rows % lateral + EDGE
    index = jnp.where(slot[None, :] < counts[:, None], place, 0)

    part, *handed = inner_planes(*fields, ylo, yhi)
    end, outgoing = rim_and_rows(index, part, xlo, xhi, handed)
    outgoing = outgoing.reshape(rows.shape + outgoing.shape[1:])
    received = lax.all_to_all(outgoing, ("gx", "gy"), split_axis=0, concat_axis=0, tiled=True)
    return end, received.reshape(-1, received.shape[-1])


def solution(mesh):
    in_specs = (
        P("gx", "gy", None),
        P("gx", "gy", None),
        P("gx", "gy", None),
        P("gx", "gy", None),
        P("gx", "gy", None, None),
        P("gx", "gy", None),
    )
    out_specs = (P("gx", "gy", None), P(("gx", "gy"), None))
    return jax.shard_map(
        per_device, mesh=mesh, in_specs=in_specs, out_specs=out_specs, check_vma=False
    )
```

```python
import functools

import jax
import jax.numpy as jnp
from jax import lax
from jax.experimental import pallas as pl
from jax.experimental.pallas import tpu as pltpu
from jax.sharding import PartitionSpec as P

STEPS = 3
TICKS = 2000
LATENT = 0.5
SHARE = 0.2
TICK_SHARE = SHARE / TICKS

HALO = 3
EDGE = 8
LEAD = 4
LANES = 128
TILE = 8
OFFSET = 2.0
FAR = 1e-30
CHUNKS = 8
OUTS = 4
UNROLL = 4
ROLL_UP = 2
ROLL_DOWN = 2
PUN = 8
RIM = 3 * HALO
HANDED = ((0, 2), (1, 2), (2, 2), (0, 4), (0, 4), (0, 4), (0, 4))
MIB = 1024 * 1024
RIM_LIMIT = 24 * MIB
LIMIT = 60 * MIB

HBM = pl.BlockSpec(memory_space=pl.ANY)
VMEM = pl.BlockSpec(memory_space=pltpu.VMEM)
SMEM = pl.BlockSpec(memory_space=pltpu.SMEM)


def kelvin(h):
    return jnp.minimum(h, jnp.maximum(h - LATENT, 1.0))


def lifted_kelvin(h):
    return jnp.minimum(h, jnp.maximum(h - LATENT, 1.0 + OFFSET))


def standing(h, bead, birth):
    return jnp.where((birth >= 0) & (birth < STEPS * TICKS), bead, h)


def face(one, two):
    return one[2] * two[2] * pl.reciprocal(one[1] + two[1], approx=True) * (two[0] - one[0])


def tile(j):
    return pl.ds(j * TILE, TILE)


class Slab:
    def __init__(self, raw, grids, rings, acc):
        self.raw = raw
        self.ha, self.hb, self.ks, self.kz, self.bs, self.bz = grids
        self.rings = rings
        self.acc = acc
        self.height = raw[0].shape[1]
        self.span = (self.height - 2 * (EDGE - LEAD)) // TILE

    def natural(self, j):
        return pl.ds(EDGE - LEAD + j, TILE, stride=self.span)

    def place(self, h, k, birth, x, rows):
        inside = k > 0.0
        values = (h, jnp.where(inside, k, 1.0), h, jnp.where(inside, birth, 1e6).astype(jnp.int32))
        for ref, value in zip(self.raw, values):
            ref[x, rows, :] = value

    def prepare(self, x, to_x):
        h_v, k_v, bead_v, birth_v = self.raw
        top = lax.broadcasted_iota(jnp.int32, (TILE, LANES), 1) == LANES - 1
        for j in range(self.span):
            at, to = self.natural(j), tile(j)
            birth, k = birth_v[x, at, :], k_v[x, at, :]
            b = birth.astype(jnp.float32) * TICK_SHARE
            self.ha[to_x, to, :] = standing(h_v[x, at, :], bead_v[x, at, :], birth) + OFFSET
            self.ks[to_x, to, :] = k
            self.kz[to_x, to, :] = jnp.where(top, FAR, pltpu.roll(k, LANES - 1, 1))
            self.bs[to_x, to, :] = b
            self.bz[to_x, to, :] = pltpu.roll(b, LANES - 1, 1)

    def prepare_all(self, lo, hi):
        @pl.loop(0, (hi - lo) // PUN)
        def _(i):
            for u in range(PUN):
                self.prepare(lo + i * PUN + u, lo + i * PUN + u)

    def into(self, ref):
        def store(x, j, value):
            ref[x, tile(j), :] = value
        return store

    def run_step(self, step, src, store, base, cuts, before=None, after=None):
        span, acc, (ring_a, ring_b) = self.span, self.acc, self.rings

        def share(b):
            return jnp.clip(SHARE * (step + 1) - b, 0.0, SHARE)

        def point(x, j):
            at = tile(j)
            h = src[x, at, :]
            t = lifted_kelvin(h)
            return h, (t, pl.reciprocal(self.ks[x, at, :] * t, approx=True), share(self.bs[x, at, :]))

        def put(ring, j, values):
            for ref, value in zip(ring, values):
                ref[tile(j), :] = value

        def get(ring, j):
            return [ref[tile(j), :] for ref in ring]

        if before is not None:
            before(0)
        for j in range(span):
            last = point(base + cuts[0] - 1, j)[1]
            h, now = point(base + cuts[0], j)
            put(ring_a, j, now)
            acc[tile(j), :] = h - face(last, now)

        def planes(xs, rings):
            slots = []

            def load(x, here, there, j):
                cur = get(here, j)
                slot = dict(x=x, j=j, cur=cur, up=pltpu.roll(cur[0], LANES - 1, 1))
                if j == 0:
                    slot["beyond"] = [pltpu.roll(v, TILE - 1, 0) for v in cur]
                    slot["fy_old"] = pltpu.roll(face(get(here, span - 1), slot["beyond"]), 1, 0)
                slot["h"], slot["nxt"] = point(x + 1, j)
                put(there, j, slot["nxt"])
                return slot

            def work(n):
                slot = slots[n]
                x, j, cur, t = slot["x"], slot["j"], slot["cur"], slot["up"]
                at = tile(j)
                fx = face(cur, slot["nxt"])
                total = acc[at, :] + fx
                acc[at, :] = slot["h"] - fx
                last = j + 1 == span
                fy = face(cur, slots[n - j]["beyond"] if last else slots[n + 1]["cur"])
                if not last:
                    slots[n + 1]["fy_old"] = fy
                fz = face(
                    cur, (t, pl.reciprocal(self.kz[x, at, :] * t, approx=True), share(self.bz[x, at, :]))
                )
                slot["total"] = total + ((fy - slot["fy_old"]) + fz)
                slot["down"] = pltpu.roll(fz, 1, 1)

            def done(n):
                slot = slots[n]
                store(slot["x"], slot["j"], slot["total"] - slot["down"])

            todo = [(x, *pair, j) for x, pair in zip(xs, rings) for j in range(span)]
            for n in range(len(todo) + ROLL_UP + ROLL_DOWN):
                if n < len(todo):
                    slots.append(load(*todo[n]))
                if 0 <= n - ROLL_UP < len(todo):
                    work(n - ROLL_UP)
                if 0 <= n - ROLL_UP - ROLL_DOWN:
                    done(n - ROLL_UP - ROLL_DOWN)

        both = [(ring_a, ring_b), (ring_b, ring_a)]
        for n, (lo, hi) in enumerate(zip(cuts[:-1], cuts[1:])):
            if hi - lo == HALO:
                planes([base + x for x in range(lo, hi)], (both * HALO)[:HALO])
                continue
            unroll = UNROLL if (hi - lo) % UNROLL == 0 else 2
            if n and before is not None:
                before(n)

            @pl.loop(0, (hi - lo) // unroll)
            def _(i):
                planes([base + lo + unroll * i + u for u in range(unroll)], both * (unroll // 2))

            if after is not None:
                after(n)


def slab_scratch(raw_planes, planes, lateral, stack, sides=None):
    tiles = (lateral + 2 * LEAD, stack)
    raw = (raw_planes, lateral + 2 * EDGE, stack)
    rings, acc = [[pltpu.VMEM(tiles, jnp.float32)] * 3] * 2, pltpu.VMEM(tiles, jnp.float32)
    return [
        [pltpu.VMEM(raw, dtype) for dtype in (jnp.float32, jnp.float32, jnp.float32, jnp.int32)],
        [pltpu.VMEM((planes,) + tiles, jnp.float32)] * 6,
        [rings] * sides if sides else rings,
        [acc] * sides if sides else acc,
    ]


def lateral_kernel(h_hbm, k_hbm, bead_hbm, birth_hbm, lo_ref, hi_ref, ys, sem):
    track, lateral, _ = h_hbm.shape
    copies = [
        pltpu.make_async_copy(hbm.at[:, pl.ds(side * (lateral - EDGE), EDGE)], ys[i].at[side], sem.at[i, side])
        for i, hbm in enumerate((h_hbm, k_hbm, bead_hbm, birth_hbm)) for side in range(2)
    ]
    for copy in copies:
        copy.start()
    for copy in copies:
        copy.wait()
    flat = [ref.reshape(2 * track * EDGE, LANES) for ref in ys]
    for side, out in ((0, lo_ref), (1, hi_ref)):
        for i in range(track // TILE):
            for d in range(HALO):
                row = (side * track + i * TILE) * EDGE + d + side * (EDGE - HALO)
                h, k, bead, birth = [ref[pl.ds(row, TILE, stride=EDGE), :] for ref in flat]
                out[d, tile(i), :] = standing(h, bead, birth)
                out[HALO + d, tile(i), :] = k
                out[2 * HALO + d, tile(i), :] = birth.astype(jnp.float32)


def track_kernel(h_hbm, k_hbm, bead_hbm, birth_hbm, lo_ref, hi_ref, xs, sem):
    track, lateral, _ = h_hbm.shape
    copies = [
        pltpu.make_async_copy(hbm.at[pl.ds(side * (track - HALO), HALO)], xs[i].at[side], sem.at[i, side])
        for i, hbm in enumerate((h_hbm, k_hbm, bead_hbm, birth_hbm)) for side in range(2)
    ]
    for copy in copies:
        copy.start()
    for copy in copies:
        copy.wait()
    rows = pl.ds(0, lateral)
    for side, out in ((0, lo_ref), (1, hi_ref)):
        @pl.loop(0, HALO)
        def _(d, side=side, out=out):
            birth = xs[3][side, d]
            out[d, rows, :] = standing(xs[0][side, d], xs[2][side, d], birth)
            out[HALO + d, rows, :] = xs[1][side, d]
            out[2 * HALO + d, rows, :] = birth.astype(jnp.float32)


def strips(kernel, fields, length, held):
    stack = fields[0].shape[2]
    out = jax.ShapeDtypeStruct((3 * HALO, length, stack), jnp.float32)
    return pl.pallas_call(
        kernel,
        out_shape=(out, out),
        in_specs=[HBM] * 4,
        out_specs=(VMEM,) * 2,
        scratch_shapes=[
            [pltpu.VMEM((2,) + held, field.dtype) for field in fields],
            pltpu.SemaphoreType.DMA((4, 2)),
        ],
        compiler_params=pltpu.CompilerParams(vmem_limit_bytes=LIMIT),
    )(*fields)


def corner_kernel(low_in, high_in, ylo_ref, yhi_ref, low_out, high_out, held, sem):
    del low_in, high_in
    track = ylo_ref.shape[1]
    copies = []
    for side, out in ((0, low_out), (1, high_out)):
        for f in range(3):
            for d in range(HALO):
                at = pl.ds(side * (track - HALO) + d, 1)
                for y, ref in enumerate((ylo_ref, yhi_ref)):
                    for e in range(HALO):
                        held[side, f * HALO + d, pl.ds(y * HALO + e, 1), :] = ref[f * HALO + e, at, :]
        rows = pl.ds(out.shape[1] - EDGE, EDGE)
        copies.append(pltpu.make_async_copy(held.at[side], out.at[:, rows], sem.at[side]))
        copies[-1].start()
    for copy in copies:
        copy.wait()


def corners(low, high, ylo, yhi):
    return pl.pallas_call(
        corner_kernel,
        out_shape=(jax.ShapeDtypeStruct(low.shape, low.dtype),) * 2,
        in_specs=[HBM] * 2 + [VMEM] * 2,
        out_specs=(HBM,) * 2,
        input_output_aliases={0: 0, 1: 1},
        scratch_shapes=[
            pltpu.VMEM((2, 3 * HALO, EDGE, LANES), jnp.float32),
            pltpu.SemaphoreType.DMA((2,)),
        ],
        compiler_params=pltpu.CompilerParams(vmem_limit_bytes=8 * MIB),
    )(low, high, ylo, yhi)


def inner_kernel(
    h_hbm, k_hbm, bead_hbm, birth_hbm, ylo_ref, yhi_ref, out_hbm, *rest
):
    handed, (raw, grids, rings, acc, sem_in, sem_out, sem_hand) = rest[:7], rest[7:]
    track, lateral, _ = h_hbm.shape
    slab = Slab(raw, grids, rings, acc)
    inner = pl.ds(EDGE, lateral)
    piece = track // CHUNKS

    def copies(n):
        at = pl.ds(n * piece, piece)
        return [
            pltpu.make_async_copy(hbm.at[at], vmem.at[at, inner], sem_in.at[i, n])
            for i, (hbm, vmem) in enumerate(zip((h_hbm, k_hbm, bead_hbm, birth_hbm), raw))
        ]

    for n in range(CHUNKS):
        for copy in copies(n):
            copy.start()

    height = lateral + 2 * EDGE
    flat = [ref.reshape(track * height, LANES) for ref in raw]
    for ref, first in ((ylo_ref, EDGE - HALO), (yhi_ref, EDGE + lateral)):
        @pl.loop(0, track // TILE)
        def _(i, ref=ref, first=first):
            for d in range(HALO):
                h, k, birth = [ref[f * HALO + d, pl.ds(i * TILE, TILE), :] for f in range(3)]
                at = pl.ds(i * TILE * height + first + d, TILE, stride=height)
                inside = k > 0.0
                flat[0][at, :] = h
                flat[1][at, :] = jnp.where(inside, k, 1.0)
                flat[2][at, :] = h
                flat[3][at, :] = jnp.where(inside, birth, 1e6).astype(jnp.int32)

    def arrive(n):
        for copy in copies(n):
            copy.wait()
        slab.prepare_all(n * piece, (n + 1) * piece)

    cuts = [HALO] + [n * (track // OUTS) + HALO for n in range(1, OUTS)] + [track - HALO]

    def out_copy(n):
        at = pl.ds(cuts[n], cuts[n + 1] - cuts[n])
        return pltpu.make_async_copy(raw[0].at[at, inner], out_hbm.at[at], sem_out.at[n])

    def finish(x, j, value):
        raw[0][x, slab.natural(j), :] = value - OFFSET

    arrivals = [1] + [n * piece - 1 for n in range(1, CHUNKS + 1)]
    def hand(i):
        ref, (first, count) = (slab.ha, slab.hb, slab.ha, *grids[2:])[i], HANDED[i]
        return [
            pltpu.make_async_copy(
                ref.at[pl.ds((first, track - first - count)[side], count)], handed[i].at[side], sem_hand.at[i, side]
            )
            for side in range(2)
        ]

    slab.run_step(0, slab.ha, slab.into(slab.hb), 0, arrivals, before=arrive)
    for i in (0, 1, 3, 4, 5, 6):
        for copy in hand(i):
            copy.start()
    slab.run_step(1, slab.hb, slab.into(slab.ha), 0, (2, track - 2))
    for copy in hand(2):
        copy.start()
    slab.run_step(2, slab.ha, finish, 0, cuts, after=lambda n: out_copy(n).start())
    for n in range(OUTS):
        out_copy(n).wait()
    for i in range(len(HANDED)):
        for copy in hand(i):
            copy.wait()


def inner_planes(h, k, bead, birth, ylo, yhi):
    track, lateral, stack = h.shape
    return pl.pallas_call(
        inner_kernel,
        out_shape=(
            jax.ShapeDtypeStruct(h.shape, jnp.float32),
            *[jax.ShapeDtypeStruct((2, n, lateral + 2 * LEAD, stack), jnp.float32) for _, n in HANDED],
        ),
        in_specs=[HBM] * 4 + [VMEM] * 2,
        out_specs=(HBM,) * (1 + len(HANDED)),
        scratch_shapes=slab_scratch(track, track, lateral, stack) + [
            pltpu.SemaphoreType.DMA((4, CHUNKS)),
            pltpu.SemaphoreType.DMA((OUTS,)),
            pltpu.SemaphoreType.DMA((len(HANDED), 2)),
        ],
        compiler_params=pltpu.CompilerParams(vmem_limit_bytes=50 * MIB),
        cost_estimate=pl.CostEstimate(
            flops=200 * h.size, bytes_accessed=20 * h.size, transcendentals=15 * h.size
        ),
    )(h, k, bead, birth, ylo, yhi)


def rim_kernel(index_ref, part_hbm, xlo_ref, xhi_ref, *rest):
    handed, (out_hbm, rows_ref, raw, grids, rings, acc, whole, sem_in, sem_part, sem_out) = rest[:7], rest[7:]
    track, lateral, _ = part_hbm.shape
    slab = Slab(raw, grids, None, None)
    inner = pl.ds(EDGE, lateral)
    own = RIM - HALO

    copies = []
    for i, (first, count) in enumerate(HANDED):
        ref = (slab.ha, slab.hb, slab.ha, *grids[2:])[i]
        for side in range(2):
            dst = (HALO + first, RIM + own - first - count)[side]
            copies.append(
                pltpu.make_async_copy(handed[i].at[side], ref.at[pl.ds(dst, count)], sem_in.at[i, side])
            )
    for copy in copies:
        copy.start()
    middle = pl.ds(HALO, track - 2 * HALO)
    part = pltpu.make_async_copy(part_hbm.at[middle], whole.at[middle, inner], sem_part)
    part.start()

    below, above = pl.ds(EDGE - HALO, HALO), pl.ds(EDGE + lateral, HALO)
    for side, ref in ((0, xlo_ref), (1, xhi_ref)):
        for d in range(HALO):
            for first, n, rows in ((0, lateral, inner), (lateral, HALO, below), (lateral + HALO, HALO, above)):
                slab.place(*[ref[f * HALO + d, pl.ds(first, n), :] for f in range(3)], side * HALO + d, rows)
    for side in range(2):
        for d in range(HALO):
            slab.prepare(side * HALO + d, side * (RIM + own) + d)
    for copy in copies:
        copy.wait()

    def finish(x, j, value):
        at = x - HALO + (track - 2 * own if x >= RIM else 0)
        whole[at, slab.natural(j), :] = value - OFFSET

    sides = [Slab(raw, grids, rings[side], acc[side]) for side in range(2)]
    stores = (slab.into(slab.hb), slab.into(slab.ha), finish)
    for step, (src, store) in enumerate(zip((slab.ha, slab.hb, slab.ha), stores)):
        for side in range(2):
            first = (1 + step, 2 * RIM - 1 - step - HALO)[side]
            sides[side].run_step(step, src, store, 0, (first, first + HALO))

    outs = []
    for side in range(2):
        at = pl.ds(side * (track - HALO), HALO)
        outs.append(pltpu.make_async_copy(whole.at[at, inner], out_hbm.at[at], sem_out.at[side]))
    for copy in outs:
        copy.start()
    part.wait()

    whole[0, 0:EDGE, :] = jnp.zeros((EDGE, LANES), jnp.float32)
    owners, slots = index_ref.shape
    flat = whole.reshape(track * (lateral + 2 * EDGE), LANES)

    @pl.loop(0, owners // 2)
    def _(i):
        for o in (2 * i, 2 * i + 1):
            for k in range(slots):
                rows_ref[pl.ds(o * slots + k, 1), :] = kelvin(flat[pl.ds(index_ref[o, k], 1), :])

    for copy in outs:
        copy.wait()


def rim_and_rows(index, part, xlo, xhi, handed):
    track, lateral, stack = part.shape
    owners, slots = index.shape
    return pl.pallas_call(
        rim_kernel,
        out_shape=(
            jax.ShapeDtypeStruct(part.shape, jnp.float32),
            jax.ShapeDtypeStruct((owners * slots, stack), jnp.float32),
        ),
        in_specs=[SMEM, HBM] + [VMEM] * 2 + [HBM] * len(HANDED),
        out_specs=(HBM, VMEM),
        input_output_aliases={1: 0},
        scratch_shapes=slab_scratch(2 * HALO, 2 * RIM, lateral, stack, 2) + [
            pltpu.VMEM((track, lateral + 2 * EDGE, stack), jnp.float32),
            pltpu.SemaphoreType.DMA((len(HANDED), 2)),
            pltpu.SemaphoreType.DMA,
            pltpu.SemaphoreType.DMA((2,)),
        ],
        compiler_params=pltpu.CompilerParams(vmem_limit_bytes=RIM_LIMIT),
        cost_estimate=pl.CostEstimate(
            flops=30 * part.size, bytes_accessed=3 * part.size, transcendentals=3 * part.size
        ),
    )(index, part, xlo, xhi, *handed)


def shift(axis, by):
    count = lax.axis_size(axis)
    return [(i, i + by) for i in range(count) if 0 <= i + by < count]


def per_device(enthalpy, conductivity, bead_enthalpy, birth_time, send_rows, send_counts):
    fields = (enthalpy, conductivity, bead_enthalpy, birth_time)

    track, lateral, stack = enthalpy.shape
    to_left, to_right = strips(lateral_kernel, fields, track, (track, EDGE, stack))
    to_low, to_high = strips(track_kernel, fields, lateral + EDGE, (HALO, lateral, stack))
    ylo = lax.ppermute(to_right, "gy", shift("gy", 1))
    yhi = lax.ppermute(to_left, "gy", shift("gy", -1))

    to_low, to_high = corners(to_low, to_high, ylo, yhi)
    xlo = lax.ppermute(to_high, "gx", shift("gx", 1))
    xhi = lax.ppermute(to_low, "gx", shift("gx", -1))

    rows, counts = send_rows[0, 0], send_counts[0, 0]
    slot = jnp.arange(rows.shape[1], dtype=jnp.int32)
    place = rows // lateral * (lateral + 2 * EDGE) + rows % lateral + EDGE
    index = jnp.where(slot[None, :] < counts[:, None], place, 0)

    part, *handed = inner_planes(*fields, ylo, yhi)
    end, outgoing = rim_and_rows(index, part, xlo, xhi, handed)
    outgoing = outgoing.reshape(rows.shape + outgoing.shape[1:])
    received = lax.all_to_all(outgoing, ("gx", "gy"), split_axis=0, concat_axis=0, tiled=True)
    return end, received.reshape(-1, received.shape[-1])


def solution(mesh):
    in_specs = (
        P("gx", "gy", None),
        P("gx", "gy", None),
        P("gx", "gy", None),
        P("gx", "gy", None),
        P("gx", "gy", None, None),
        P("gx", "gy", None),
    )
    out_specs = (P("gx", "gy", None), P(("gx", "gy"), None))
    return jax.shard_map(
        per_device, mesh=mesh, in_specs=in_specs, out_specs=out_specs, check_vma=False
    )
```
